256 devices in a mesh: row: 4 (over x_hi, core), rad: 2 (over x_lo), azi: 32 (over z, y).
Axes of the slice: x: 4 (x_hi: 2, x_lo: 2; x = x_hi * 2 + x_lo), y: 4, z: 8, core: 2. Of those that a mesh axis runs over, the one named last changes fastest.
Arguments:
- density: float32 [64, 32, 8192], P('row', 'rad', 'azi'), may hold values from 0.8 to 1.25
- velocity: float32 [3, 64, 32, 8192], P(None, 'row', 'rad', 'azi'), may hold values from -1.2 to 1.2
- pressure: float32 [64, 32, 8192], P('row', 'rad', 'azi'), may hold values from 0.6 to 1.4
- nu_tilde: float32 [64, 32, 8192], P('row', 'rad', 'azi'), may hold values from 0.02 to 0.2
- wall_distance: float32 [64, 32, 8192], P('row', 'rad', 'azi'), may hold values from 0.5 to 4
- interp_fwd: float32 [32, 32], P('rad')
- interp_back: float32 [32, 32], P('rad')
- offset: int32 [1], replicated, may hold values from 0 to 8191
Outputs:
- flow_next: float32 [6, 64, 32, 8192], P(None, 'row', 'rad', 'azi')
- shielding: float32 [64, 32, 8192], P('row', 'rad', 'azi')
The draws below stay inside these ranges and needn't reach their ends.
All inputs are finite; a program needn't handle non-finite values.
Results may differ from the reference program's by a relative error of at most 0.00005.
Values sent between devices are 32-bit elements; how exact they have to be, the bound alone decides.
No kernel may reach another device: no remote copies, remote signals or barrier semaphores. Data moves between devices by JAX's collectives and lax.ppermute only.
A program may use at most 128 MiB of HBM per device.

```python
import math
import jax
import jax.numpy as jnp
from jax import lax

NA = 64
NR = 32
NT = 8192


def weights_table(key, count):
    spread = jax.random.uniform(key, (count, count), jnp.float32, 0.0, 1.0)
    return 0.5 * jnp.eye(count, dtype=jnp.float32) + spread * (1.0 / count)


def draw_interp_fwd(key, part):
    key = jax.random.fold_in(key, 11)
    return weights_table(key, NR)


def draw_interp_back(key, part):
    key = jax.random.fold_in(key, 23)
    return weights_table(key, NR)


def shard_levels(key, shape, split, low, largest):
    loudness = 1.0
    for position, blocks in split:
        steps = jax.random.uniform(jax.random.fold_in(jax.random.fold_in(key, 6), position), (blocks,), jnp.float32, low / len(split), largest / len(split))
        loudness = loudness * jnp.repeat(jnp.exp(steps), shape[position] // blocks).reshape((-1,) + (1,) * (len(shape) - 1 - position))
    return loudness


def gaussian(stream_key, dims, deviation, limit, shards=(), held_as=jnp.bfloat16):
    values = deviation * jax.random.normal(stream_key, dims, jnp.float32)
    if shards:
        values = values * shard_levels(stream_key, dims, shards, -0.22, 0.18)
    return jnp.clip(values, -limit, limit).astype(held_as)


def setup_inputs(seed: int = 0) -> dict:
    streams_of = jax.random.split(jax.random.key(seed), 9)
    density = jnp.clip(0.8 + 0.45 * jax.random.uniform(streams_of[0], (NA, NR, NT), jnp.float32) ** shard_levels(streams_of[0], (NA, NR, NT), ((0, 4), (1, 2), (2, 32)), -0.2, 0.2), 0.8, 1.25)
    velocity = gaussian(streams_of[1], (3, NA, NR, NT), 0.3, 1.2, ((1, 4), (2, 2), (3, 32)), jnp.float32)
    pressure = jnp.clip(0.6 + 0.79999995 * jax.random.uniform(streams_of[2], (NA, NR, NT), jnp.float32) ** shard_levels(streams_of[2], (NA, NR, NT), ((0, 4), (1, 2), (2, 32)), -0.2, 0.2), 0.6, 1.4)
    nu_tilde = jnp.clip(jnp.exp(math.log(0.2) - 2.3025851 * jax.random.uniform(streams_of[3], (NA, NR, NT), jnp.float32) ** shard_levels(streams_of[3], (NA, NR, NT), ((0, 4), (1, 2), (2, 32)), -0.2, 0.2)), 0.02, 0.2)
    wall_distance = jnp.clip(jnp.exp(math.log(4.0) - 2.0794415 * jax.random.uniform(streams_of[4], (NA, NR, NT), jnp.float32) ** shard_levels(streams_of[4], (NA, NR, NT), ((0, 4), (1, 2), (2, 32)), -0.2, 0.2)), 0.5, 4.0)
    interp_fwd = draw_interp_fwd(jax.random.fold_in(streams_of[8], 71), 0)
    interp_back = draw_interp_back(jax.random.fold_in(streams_of[8], 71), 0)
    offset = jax.random.randint(streams_of[7], (1,), 0, NT).astype(jnp.int32)
    return dict(density=density, velocity=velocity, pressure=pressure, nu_tilde=nu_tilde, wall_distance=wall_distance, interp_fwd=interp_fwd, interp_back=interp_back, offset=offset)


GAMMA = 1.4
CFL = 0.8
KAPPA = 0.41
C_DES = 0.65
CB1 = 0.1355
CW1 = 3.239
NU_LAM = 0.001
GRAD_FLOOR = 0.2

def conserved(prim):
    rho = prim[0]
    energy = prim[4] / (GAMMA - 1.0) + 0.5 * rho * (prim[1] ** 2 + prim[2] ** 2 + prim[3] ** 2)
    return jnp.stack([rho, rho * prim[1], rho * prim[2], rho * prim[3], energy, rho * prim[5]], 0)

def normal_flux(prim, direction):
    cons = conserved(prim)
    normal = prim[1 + direction]
    press = prim[4]
    flux = cons * normal[None]
    extra = [jnp.zeros_like(press)] * 6
    extra[1 + direction] = press
    extra[4] = press * normal
    flux = flux + jnp.stack(extra, 0)
    speed = jnp.abs(normal) + jnp.sqrt(GAMMA * press / prim[0])
    return (cons, flux, speed)

def rusanov(left, right, direction):
    cons_l, flux_l, speed_l = normal_flux(left, direction)
    cons_r, flux_r, speed_r = normal_flux(right, direction)
    return 0.5 * (flux_l + flux_r) - 0.5 * jnp.maximum(speed_l, speed_r)[None] * (cons_r - cons_l)

def divergence(padded, direction, axis):
    count = padded.shape[axis]
    left = lax.slice_in_dim(padded, 0, count - 1, axis=axis)
    right = lax.slice_in_dim(padded, 1, count, axis=axis)
    faces = rusanov(left, right, direction)
    return lax.slice_in_dim(faces, 1, count - 1, axis=axis) - lax.slice_in_dim(faces, 0, count - 2, axis=axis)

def grad_squares(padded, axis):
    count = padded.shape[axis]
    upper = lax.slice_in_dim(padded[1:4], 2, count, axis=axis)
    lower = lax.slice_in_dim(padded[1:4], 0, count - 2, axis=axis)
    return lax.optimization_barrier(jnp.sum((0.5 * (upper - lower)) ** 2, axis=0))

def speed_bound(prim):
    return jnp.abs(prim[1]) + jnp.abs(prim[2]) + jnp.abs(prim[3]) + 3.0 * jnp.sqrt(GAMMA * prim[4] / prim[0])

def wall_pad(prim, lower, upper):
    return jnp.concatenate([lower[:, :, None], prim, upper[:, :, None]], 2)

def update(prim, flux_sum, grad2, wall_distance, step_size):
    rho = prim[0]
    nut = prim[5]
    strain = jnp.maximum(jnp.sqrt(grad2), GRAD_FLOOR)
    ratio = (nut + NU_LAM) / (KAPPA * KAPPA * wall_distance * wall_distance * strain)
    shielding = 1.0 - jnp.tanh((8.0 * ratio) ** 3)
    length = wall_distance - shielding * jnp.maximum(0.0, wall_distance - C_DES)
    source = rho * (CB1 * strain * nut - CW1 * (nut / length) ** 2)
    state = conserved(prim) - step_size * flux_sum
    state = jnp.concatenate([state[:5], (state[5] + step_size * source)[None]], 0)
    return (state, shielding)

def roll_cycle(plane, amount, total):
    index = (jnp.arange(total, dtype=jnp.int32) - amount) % total
    return jnp.take(plane, index, axis=2)

def reference(density, velocity, pressure, nu_tilde, wall_distance, interp_fwd, interp_back, offset):
    prim = jnp.concatenate([density[None], velocity, pressure[None], nu_tilde[None]], 0)
    middle = NA // 2
    shift_total = offset[0]
    ghost_fwd = jnp.einsum('rk,vkt->vrt', interp_fwd, roll_cycle(prim[:, middle - 1], shift_total, NT), precision=lax.Precision.HIGHEST)
    ghost_back = jnp.einsum('rk,vkt->vrt', interp_back, roll_cycle(prim[:, middle], (NT - shift_total) % NT, NT), precision=lax.Precision.HIGHEST)
    rotor = prim[:, :middle]
    stator = prim[:, middle:]
    rotor_pad = jnp.concatenate([rotor[:, :1], rotor, ghost_back[:, None]], 1)
    stator_pad = jnp.concatenate([ghost_fwd[:, None], stator, stator[:, -1:]], 1)
    flip = jnp.array([1.0, 1.0, -1.0, 1.0, 1.0, 1.0], dtype=jnp.float32).reshape(6, 1, 1)
    radial_pad = wall_pad(prim, prim[:, :, 0] * flip, prim[:, :, -1] * flip)
    cycle_pad = jnp.concatenate([prim[..., -1:], prim, prim[..., :1]], 3)
    flux_sum = jnp.concatenate([divergence(rotor_pad, 0, 1), divergence(stator_pad, 0, 1)], 1)
    flux_sum = flux_sum + divergence(radial_pad, 1, 2) + divergence(cycle_pad, 2, 3)
    grad2 = jnp.concatenate([grad_squares(rotor_pad, 1), grad_squares(stator_pad, 1)], 0)
    grad2 = grad2 + grad_squares(radial_pad, 2) + grad_squares(cycle_pad, 3)
    step_size = CFL / jnp.max(speed_bound(prim))
    return update(prim, flux_sum, grad2, wall_distance, step_size)
```

```python
import functools

import jax
import jax.numpy as jnp
from jax import lax
from jax.experimental import pallas as pl
from jax.experimental.pallas import tpu as pltpu
from jax.sharding import PartitionSpec as P

GAMMA = 1.4
CFL = 0.8
KAPPA = 0.41
C_DES = 0.65
CB1 = 0.1355
CW1 = 3.239
NU_LAM = 0.001
GRAD_FLOOR = 0.2

AXES = ("row", "rad", "azi")
LANES = 128
F32 = jnp.float32
VMEM = pl.BlockSpec(memory_space=pltpu.VMEM)
SMEM = pl.BlockSpec(memory_space=pltpu.SMEM)


def params(mib=48):
    return pltpu.CompilerParams(vmem_limit_bytes=mib * 1024 * 1024)


def shaped(*dims):
    return jax.ShapeDtypeStruct(dims, F32)


def sound_speed(rho, press):
    return jnp.sqrt(GAMMA * press / rho)


def energy_of(press, m, u):
    return press * (1.0 / (GAMMA - 1.0)) + 0.5 * (m[0] * u[0] + m[1] * u[1] + m[2] * u[2])


def state_of(prim):
    rho, u, press, nut = prim[0], prim[1:4], prim[4], prim[5]
    m = [rho * v for v in u]
    return dict(
        rho=rho, m=m, u=u, p=press, e=energy_of(press, m, u), n=rho * nut, c=sound_speed(rho, press)
    )


def cons_of(s):
    return [s["rho"], s["m"][0], s["m"][1], s["m"][2], s["e"], s["n"]]


def flux_of(s, k):
    w = s["u"][k]
    mom = [s["m"][k] * s["u"][i] for i in range(3)]
    mom[k] = mom[k] + s["p"]
    return [s["m"][k], mom[0], mom[1], mom[2], (s["e"] + s["p"]) * w, s["n"] * w]


def face_of(left, right, k):
    wave = jnp.maximum(jnp.abs(left["u"][k]) + left["c"], jnp.abs(right["u"][k]) + right["c"])
    return [
        (fl + fr) - wave * (ur - ul)
        for fl, fr, ul, ur in zip(
            flux_of(left, k), flux_of(right, k), cons_of(left), cons_of(right)
        )
    ]


NAMES = ("rho", "u0", "u1", "u2", "p", "m0", "m1", "m2", "e", "n", "c")
PASSED = ("rho", "u0", "u1", "u2", "p", "e", "n", "c")


def pack_state(s):
    return dict(
        rho=s["rho"], u0=s["u"][0], u1=s["u"][1], u2=s["u"][2], p=s["p"], e=s["e"], n=s["n"], c=s["c"]
    )


def unpack_state(d):
    u = [d["u0"], d["u1"], d["u2"]]
    return dict(rho=d["rho"], u=u, m=[d["rho"] * v for v in u], p=d["p"], e=d["e"], n=d["n"], c=d["c"])


def derive_kernel(rho, vel, press, nut, der, core, outer, layer, col_up, col_down, top):
    count, radial, width = rho.shape
    even = lax.axis_index("row") % 2 == 0
    inner_rad = lax.axis_index("rad") == 0
    lane = lax.broadcasted_iota(jnp.int32, (radial, LANES), 1)

    def field(v, a):
        if v == 0:
            return rho[a]
        if v == 4:
            return press[a]
        if v == 5:
            return nut[a]
        return vel[v - 1, a]

    def step(a, best):
        r, p = rho[a], press[a]
        u = [vel[i, a] for i in range(3)]
        m = [r * v for v in u]
        c = sound_speed(r, p)
        der[0, a] = m[0]
        der[1, a] = m[1]
        der[2, a] = m[2]
        der[3, a] = energy_of(p, m, u)
        der[4, a] = r * nut[a]
        der[5, a] = c
        speed = jnp.abs(u[0]) + jnp.abs(u[1]) + jnp.abs(u[2]) + 3.0 * c
        for v in range(6):
            plane = field(v, a)
            layer[v, pl.ds(a, 1), :] = jnp.where(inner_rad, plane[radial - 1 :], plane[:1])
            first, last = plane[:, :LANES], plane[:, width - LANES :]
            here = lane == a
            col_up[v] = jnp.where(here, pltpu.roll(last, a + 1, 1), col_up[v])
            col_down[v] = jnp.where(here, pltpu.roll(first, a, 1), col_down[v])
        return jnp.maximum(best, speed)

    col_up[...] = jnp.zeros(col_up.shape, F32)
    col_down[...] = jnp.zeros(col_down.shape, F32)
    best = lax.fori_loop(0, count, step, jnp.zeros((radial, width), F32))
    for v in range(6):
        low, high = field(v, 0), field(v, count - 1)
        core[v] = jnp.where(even, high, low)
        outer[v] = jnp.where(even, low, high)
    largest = jnp.max(best, axis=0, keepdims=True)
    largest = jnp.max(largest, axis=1, keepdims=True)
    top[...] = jnp.broadcast_to(largest.reshape(1, 1, 1), top.shape)


def shift_kernel(cycle, shift, before, own, out):
    width = own.shape[2]
    row = lax.axis_index("row")
    amount = shift[0] % width
    amount = jnp.where(row == 1, amount, jnp.where(row == 2, width - amount, 0))
    tiles = amount // LANES
    rest = amount % LANES
    lane = lax.broadcasted_iota(jnp.int32, (own.shape[1], LANES), 1)
    for v in range(6):
        parts = [
            pltpu.roll(ref[v, :, h * LANES : (h + 1) * LANES], rest, 1)
            for ref in (before, own)
            for h in range(2)
        ]
        for t in range(2):
            picks = [
                jnp.where(lane < rest, parts[max(1 + t - q, 0)], parts[2 + t - q]) for q in range(3)
            ]
            out[v, :, t * LANES : (t + 1) * LANES] = jnp.where(
                tiles == 0, picks[0], jnp.where(tiles == 1, picks[1], picks[2])
            )


def weight_kernel(fwd, back, own, other, out):
    width = own.shape[2]
    radial = own.shape[1]
    low = lax.axis_index("rad") == 0
    table = jnp.where(lax.axis_index("row") == 1, fwd[...], back[...])
    for v in range(6):
        first = jnp.where(low, own[v], other[v])
        second = jnp.where(low, other[v], own[v])
        plane = jnp.concatenate([first, second], 0)
        out[v] = jnp.dot(
            table, plane, precision=lax.Precision.HIGHEST, preferred_element_type=F32
        )


def main_kernel(
    rho, vel, press, nut, der, wall, core, ghost, outer, layer, col_prev, col_next, col_own, top,
    flow, shield, low_face, lay_hi, lay_lo, lay_u, azi_hi, azi_lo, azi_u,
):
    count, radial, width = rho.shape
    row, rad = lax.axis_index("row"), lax.axis_index("rad")
    even = row % 2 == 0
    at_low = rad == 0
    coupled = (row == 1) | (row == 2)
    sub = lax.broadcasted_iota(jnp.int32, (8, width), 0)
    lane = lax.broadcasted_iota(jnp.int32, (radial, LANES), 1)
    step_size = CFL / jnp.max(top[...])
    half = 0.5 * step_size

    def prims(a):
        return [rho[a], vel[0, a], vel[1, a], vel[2, a], press[a], nut[a]]

    def state_at(a):
        return dict(
            rho=rho[a],
            u=[vel[i, a] for i in range(3)],
            p=press[a],
            m=[der[i, a] for i in range(3)],
            e=der[3, a],
            n=der[4, a],
            c=der[5, a],
        )

    def up_r(v, halo):
        lo, hi = pltpu.roll(v[:8], 7, 0), pltpu.roll(v[8:], 7, 0)
        edge = sub == 7
        return jnp.concatenate([jnp.where(edge, hi, lo), jnp.where(edge, halo, hi)], 0)

    def down_r(v, halo):
        lo, hi = pltpu.roll(v[:8], 1, 0), pltpu.roll(v[8:], 1, 0)
        edge = sub == 0
        return jnp.concatenate([jnp.where(edge, halo, lo), jnp.where(edge, lo, hi)], 0)

    def up_t(v, halo):
        lo, hi = pltpu.roll(v[:, :LANES], LANES - 1, 1), pltpu.roll(v[:, LANES:], LANES - 1, 1)
        edge = lane == LANES - 1
        return jnp.concatenate([jnp.where(edge, hi, lo), jnp.where(edge, halo, hi)], 1)

    def down_t(v, halo):
        lo, hi = pltpu.roll(v[:, :LANES], 1, 1), pltpu.roll(v[:, LANES:], 1, 1)
        edge = lane == 0
        return jnp.concatenate([jnp.where(edge, halo, lo), jnp.where(edge, lo, hi)], 1)

    def edge_layer(r):
        return [rho[:, r, :], vel[0, :, r, :], vel[1, :, r, :], vel[2, :, r, :], press[:, r, :], nut[:, r, :]]

    def mirrored(prim):
        return [prim[0], prim[1], -prim[2], prim[3], prim[4], prim[5]]

    got = [layer[v] for v in range(6)]
    bottom, ceiling = edge_layer(0), edge_layer(radial - 1)
    high = [jnp.where(at_low, g, w) for g, w in zip(got, mirrored(ceiling))]
    low = [jnp.where(at_low, w, g) for g, w in zip(got, mirrored(bottom))]
    high_state = pack_state(state_of(high))
    for i, name in enumerate(PASSED):
        lay_hi[i] = high_state[name]
    for i, f in enumerate(face_of(state_of(low), state_of(bottom), 1)):
        lay_lo[i] = f
    for i in range(3):
        lay_u[i] = low[1 + i]

    nxt = state_of([col_next[v] for v in range(6)])
    nxt_state = pack_state(nxt)
    for i, name in enumerate(PASSED):
        azi_hi[i] = nxt_state[name]
    prev = [col_prev[v] for v in range(6)]
    for i, f in enumerate(face_of(state_of(prev), state_of([col_own[v] for v in range(6)]), 2)):
        azi_lo[i] = f
    for i in range(3):
        azi_u[i] = prev[1 + i]

    def end_prims(is_core, a):
        return [
            jnp.where(is_core, core[v], jnp.where(coupled, ghost[v], outer[v])) for v in range(6)
        ]

    below = end_prims(jnp.logical_not(even), 0)
    above = end_prims(even, count - 1)
    for i, f in enumerate(face_of(state_of(below), state_at(0), 0)):
        low_face[i] = f

    def step(a, _):
        here = state_at(a)
        nut_a = nut[a]
        last = a == count - 1
        first = a == 0
        later = jnp.minimum(a + 1, count - 1)
        earlier = jnp.maximum(a - 1, 0)
        up_prims = [jnp.where(last, g, h) for g, h in zip(above, prims(later))]
        total = [None] * 6
        grad2 = None
        right = state_of(up_prims)
        for i, f in enumerate(face_of(here, right, 0)):
            total[i] = f - low_face[i]
            low_face[i] = f
        for i in range(3):
            down = jnp.where(first, below[1 + i], vel[i, earlier])
            d = up_prims[1 + i] - down
            grad2 = d * d if grad2 is None else grad2 + d * d
        packed = pack_state(here)
        row_of = pl.ds(a, 1)
        shifted = {n: up_r(packed[n], lay_hi[i, row_of, :]) for i, n in enumerate(PASSED)}
        face = face_of(here, unpack_state(shifted), 1)
        for i, f in enumerate(face):
            total[i] = total[i] + (f - down_r(f, lay_lo[i, row_of, :]))
        for i in range(3):
            d = shifted["u%d" % i] - down_r(here["u"][i], lay_u[i, row_of, :])
            grad2 = grad2 + d * d
        to_end = (LANES - 1) - a
        to_start = (LANES - a) % LANES
        shifted = {n: up_t(packed[n], pltpu.roll(azi_hi[i], to_end, 1)) for i, n in enumerate(PASSED)}
        face = face_of(here, unpack_state(shifted), 2)
        for i, f in enumerate(face):
            total[i] = total[i] + (f - down_t(f, pltpu.roll(azi_lo[i], to_start, 1)))
        for i in range(3):
            d = shifted["u%d" % i] - down_t(here["u"][i], pltpu.roll(azi_u[i], to_start, 1))
            grad2 = grad2 + d * d
        dist = wall[a]
        strain = jnp.maximum(jnp.sqrt(0.25 * grad2), GRAD_FLOOR)
        ratio = (nut_a + NU_LAM) / (KAPPA * KAPPA * dist * dist * strain)
        eight = 8.0 * ratio
        shielding = 1.0 - jnp.tanh(eight * eight * eight)
        length = dist - shielding * jnp.maximum(0.0, dist - C_DES)
        quot = nut_a / length
        source = here["rho"] * (CB1 * strain * nut_a - CW1 * (quot * quot))
        cons = cons_of(here)
        for i in range(5):
            flow[i, a] = cons[i] - half * total[i]
        flow[5, a] = cons[5] - half * total[5] + step_size * source
        shield[a] = shielding
        return 0

    lax.fori_loop(0, count, step, 0)


def body(density, velocity, pressure, nu_tilde, wall_distance, interp_fwd, interp_back, offset):
    rows, rads, cycle = (lax.axis_size(n) for n in AXES)
    count, radial, width = density.shape
    devices = rows * rads * cycle

    def device(row, rad, azi):
        return (row * rads + rad) * cycle + azi % cycle

    def everyone(target):
        return [
            (device(r, d, a), target(r, d, a))
            for r in range(rows)
            for d in range(rads)
            for a in range(cycle)
        ]

    plane = shaped(6, radial, width)
    column = shaped(6, radial, LANES)
    der, core, outer, layer, col_up, col_down, top = pl.pallas_call(
        derive_kernel,
        out_shape=(
            shaped(6, count, radial, width), plane, plane, shaped(6, count, width), column, column,
            shaped(devices, 1, LANES),
        ),
        in_specs=[VMEM] * 4,
        out_specs=(VMEM,) * 7,
        compiler_params=params(),
        name="derive",
    )(density, velocity, pressure, nu_tilde)

    up = everyone(lambda r, d, a: device(r, d, a + 1))
    down = everyone(lambda r, d, a: device(r, d, a - 1))
    pair = everyone(lambda r, d, a: device(r ^ 1, d, a))
    across = everyone(lambda r, d, a: device(r, rads - 1 - d, a))
    came = lax.ppermute(jnp.concatenate([outer, col_up], 2), AXES, up)
    col_next = lax.ppermute(col_down, AXES, down)
    core_got = lax.ppermute(core, AXES, pair)
    tops = lax.all_to_all(top, AXES, 0, 0)

    moved = pl.pallas_call(
        functools.partial(shift_kernel, cycle),
        out_shape=plane,
        in_specs=[SMEM, VMEM, VMEM],
        out_specs=VMEM,
        compiler_params=params(),
        name="shift",
    )(offset, came[:, :, :width], outer)
    swapped = lax.ppermute(jnp.concatenate([moved, layer], 1), AXES, across)
    weighted = pl.pallas_call(
        weight_kernel,
        out_shape=plane,
        in_specs=[VMEM] * 4,
        out_specs=VMEM,
        compiler_params=params(),
        name="weigh",
    )(interp_fwd, interp_back, moved, swapped[:, :radial])

    def far(blocks):
        route = []
        for d in range(rads):
            for a in range(cycle):
                route.append((device(1, d, a), device(2, d, a + blocks)))
                route.append((device(2, d, a), device(1, d, a + cycle - 1 - blocks)))
        return lambda block: lax.ppermute(block, AXES, route)

    ghost = lax.switch(offset[0] // width, [far(b) for b in range(cycle)], weighted)

    return pl.pallas_call(
        main_kernel,
        out_shape=(shaped(6, count, radial, width), shaped(count, radial, width)),
        in_specs=[VMEM] * 14,
        out_specs=(VMEM, VMEM),
        scratch_shapes=[
            pltpu.VMEM((6, radial, width), F32),
            pltpu.VMEM((8, count, width), F32),
            pltpu.VMEM((6, count, width), F32),
            pltpu.VMEM((3, count, width), F32),
            pltpu.VMEM((8, radial, LANES), F32),
            pltpu.VMEM((6, radial, LANES), F32),
            pltpu.VMEM((3, radial, LANES), F32),
        ],
        compiler_params=params(),
        name="advance",
    )(
        density, velocity, pressure, nu_tilde, der, wall_distance, core_got, ghost, outer,
        swapped[:, radial:], came[:, :, width:], col_next, col_down, tops,
    )


def solution(mesh):
    placed = (
        P("row", "rad", "azi"),
        P(None, "row", "rad", "azi"),
        P("row", "rad", "azi"),
        P("row", "rad", "azi"),
        P("row", "rad", "azi"),
        P("rad", None),
        P("rad", None),
        P(),
    )
    return jax.shard_map(
        body,
        mesh=mesh,
        in_specs=placed,
        out_specs=(P(None, "row", "rad", "azi"), P("row", "rad", "azi")),
        check_vma=False,
    )
```

```python
import functools

import jax
import jax.numpy as jnp
from jax import lax
from jax.experimental import pallas as pl
from jax.experimental.pallas import tpu as pltpu
from jax.sharding import PartitionSpec as P

GAMMA = 1.4
CFL = 0.8
KAPPA = 0.41
C_DES = 0.65
CB1 = 0.1355
CW1 = 3.239
NU_LAM = 0.001
GRAD_FLOOR = 0.2

AXES = ("row", "rad", "azi")
LANES = 128
F32 = jnp.float32
VMEM = pl.BlockSpec(memory_space=pltpu.VMEM)
SMEM = pl.BlockSpec(memory_space=pltpu.SMEM)
HBM = pl.BlockSpec(memory_space=pltpu.HBM)


def params(mib=48):
    return pltpu.CompilerParams(vmem_limit_bytes=mib * 1024 * 1024)


def shaped(*dims):
    return jax.ShapeDtypeStruct(dims, F32)


def sound_speed(rho, press):
    return jnp.sqrt(GAMMA * press / rho)


def energy_of(press, m, u):
    return press * (1.0 / (GAMMA - 1.0)) + 0.5 * (m[0] * u[0] + m[1] * u[1] + m[2] * u[2])


def state_of(prim):
    rho, u, press, nut = prim[0], prim[1:4], prim[4], prim[5]
    m = [rho * v for v in u]
    return dict(
        rho=rho, m=m, u=u, p=press, e=energy_of(press, m, u), n=rho * nut, c=sound_speed(rho, press)
    )


def cons_of(s):
    return [s["rho"], s["m"][0], s["m"][1], s["m"][2], s["e"], s["n"]]


def flux_of(s, k):
    w = s["u"][k]
    mom = [s["m"][k] * s["u"][i] for i in range(3)]
    mom[k] = mom[k] + s["p"]
    return [s["m"][k], mom[0], mom[1], mom[2], (s["e"] + s["p"]) * w, s["n"] * w]


def face_of(left, right, k):
    wave = jnp.maximum(jnp.abs(left["u"][k]) + left["c"], jnp.abs(right["u"][k]) + right["c"])
    return [
        (fl + fr) - wave * (ur - ul)
        for fl, fr, ul, ur in zip(
            flux_of(left, k), flux_of(right, k), cons_of(left), cons_of(right)
        )
    ]


NAMES = ("rho", "u0", "u1", "u2", "p", "m0", "m1", "m2", "e", "n", "c")
PASSED = ("rho", "u0", "u1", "u2", "p", "e", "n", "c")


def pack_state(s):
    return dict(
        rho=s["rho"], u0=s["u"][0], u1=s["u"][1], u2=s["u"][2], p=s["p"], e=s["e"], n=s["n"], c=s["c"]
    )


def unpack_state(d):
    u = [d["u0"], d["u1"], d["u2"]]
    return dict(rho=d["rho"], u=u, m=[d["rho"] * v for v in u], p=d["p"], e=d["e"], n=d["n"], c=d["c"])


def derive_kernel(
    rho_in, vel_in, press_in, nut_in, wall_in,
    prim, der, wall, core, up_send, layer, col_down, top, sems,
):
    _, count, radial, width = prim.shape
    even = lax.axis_index("row") % 2 == 0
    inner_rad = lax.axis_index("rad") == 0
    lane = lax.broadcasted_iota(jnp.int32, (radial, LANES), 1)
    copies = [
        pltpu.make_async_copy(rho_in, prim.at[0], sems.at[0]),
        pltpu.make_async_copy(vel_in, prim.at[pl.ds(1, 3)], sems.at[1]),
        pltpu.make_async_copy(press_in, prim.at[4], sems.at[2]),
        pltpu.make_async_copy(nut_in, prim.at[5], sems.at[3]),
        pltpu.make_async_copy(wall_in, wall, sems.at[4]),
    ]
    for c in copies:
        c.start()
    up_send[:, :, width:] = jnp.zeros((6, radial, LANES), F32)
    col_down[...] = jnp.zeros(col_down.shape, F32)
    for c in copies[:4]:
        c.wait()

    def step(a, best):
        r, p = prim[0, a], prim[4, a]
        u = [prim[1 + i, a] for i in range(3)]
        m = [r * v for v in u]
        c = sound_speed(r, p)
        der[0, a] = m[0]
        der[1, a] = m[1]
        der[2, a] = m[2]
        der[3, a] = energy_of(p, m, u)
        der[4, a] = r * prim[5, a]
        der[5, a] = c
        speed = jnp.abs(u[0]) + jnp.abs(u[1]) + jnp.abs(u[2]) + 3.0 * c
        here = lane == a
        for v in range(6):
            plane = prim[v, a]
            layer[v, pl.ds(a, 1), :] = jnp.where(inner_rad, plane[radial - 1 :], plane[:1])
            first, last = plane[:, :LANES], plane[:, width - LANES :]
            up_send[v, :, width:] = jnp.where(
                here, pltpu.roll(last, a + 1, 1), up_send[v, :, width:]
            )
            col_down[v] = jnp.where(here, pltpu.roll(first, a, 1), col_down[v])
        return jnp.maximum(best, speed)

    best = lax.fori_loop(0, count, step, jnp.zeros((radial, width), F32))
    for v in range(6):
        low, high = prim[v, 0], prim[v, count - 1]
        core[v] = jnp.where(even, high, low)
        up_send[v, :, :width] = jnp.where(even, low, high)
    largest = jnp.max(best, axis=0, keepdims=True)
    largest = jnp.max(largest, axis=1, keepdims=True)
    top[...] = jnp.broadcast_to(largest.reshape(1, 1, 1), top.shape)
    copies[4].wait()


def shift_kernel(shift, came, sent, layer, out):
    radial, width = layer.shape[1], layer.shape[2]
    row = lax.axis_index("row")
    amount = shift[0] % width
    amount = jnp.where(row == 1, amount, jnp.where(row == 2, width - amount, 0))
    tiles = amount // LANES
    rest = amount % LANES
    lane = lax.broadcasted_iota(jnp.int32, (radial, LANES), 1)
    for v in range(6):
        parts = [
            pltpu.roll(ref[v, :, h * LANES : (h + 1) * LANES], rest, 1)
            for ref in (came, sent)
            for h in range(2)
        ]
        for t in range(2):
            picks = [
                jnp.where(lane < rest, parts[max(1 + t - q, 0)], parts[2 + t - q]) for q in range(3)
            ]
            out[v, :radial, t * LANES : (t + 1) * LANES] = jnp.where(
                tiles == 0, picks[0], jnp.where(tiles == 1, picks[1], picks[2])
            )
        out[v, radial:, :] = layer[v]


def weight_kernel(fwd, back, own, other, out):
    radial = out.shape[1]
    low = lax.axis_index("rad") == 0
    table = jnp.where(lax.axis_index("row") == 1, fwd[...], back[...])
    for v in range(6):
        mine, theirs = own[v, :radial], other[v, :radial]
        plane = jnp.concatenate([jnp.where(low, mine, theirs), jnp.where(low, theirs, mine)], 0)
        out[v] = jnp.dot(
            table, plane, precision=lax.Precision.HIGHEST, preferred_element_type=F32
        )


def closure(rho, nut, dist, grad2):
    strain = jnp.maximum(jnp.sqrt(0.25 * grad2), GRAD_FLOOR)
    ratio = (nut + NU_LAM) / (KAPPA * KAPPA * dist * dist * strain)
    eight = 8.0 * ratio
    shielding = 1.0 - jnp.tanh(eight * eight * eight)
    length = dist - shielding * jnp.maximum(0.0, dist - C_DES)
    quot = nut / length
    return shielding, rho * (CB1 * strain * nut - CW1 * (quot * quot))


def state_at(prim, der, a):
    return dict(
        rho=prim[0, a],
        u=[prim[1 + i, a] for i in range(3)],
        p=prim[4, a],
        m=[der[i, a] for i in range(3)],
        e=der[3, a],
        n=der[4, a],
        c=der[5, a],
    )


def face_kernel(
    prim, der, wall, core, swapped, came, col_next, col_own,
    total_out, shield, source_out, grad_out,
    low_face, lay_hi, lay_lo, lay_u, azi_hi, azi_lo, azi_u,
):
    _, count, radial, width = prim.shape
    row, rad = lax.axis_index("row"), lax.axis_index("rad")
    even = row % 2 == 0
    at_low = rad == 0
    sub = lax.broadcasted_iota(jnp.int32, (8, width), 0)
    lane = lax.broadcasted_iota(jnp.int32, (radial, LANES), 1)

    def up_r(v, halo):
        lo, hi = pltpu.roll(v[:8], 7, 0), pltpu.roll(v[8:], 7, 0)
        edge = sub == 7
        return jnp.concatenate([jnp.where(edge, hi, lo), jnp.where(edge, halo, hi)], 0)

    def down_r(v, halo):
        lo, hi = pltpu.roll(v[:8], 1, 0), pltpu.roll(v[8:], 1, 0)
        edge = sub == 0
        return jnp.concatenate([jnp.where(edge, halo, lo), jnp.where(edge, lo, hi)], 0)

    def up_t(v, halo):
        lo, hi = pltpu.roll(v[:, :LANES], LANES - 1, 1), pltpu.roll(v[:, LANES:], LANES - 1, 1)
        edge = lane == LANES - 1
        return jnp.concatenate([jnp.where(edge, hi, lo), jnp.where(edge, halo, hi)], 1)

    def down_t(v, halo):
        lo, hi = pltpu.roll(v[:, :LANES], 1, 1), pltpu.roll(v[:, LANES:], 1, 1)
        edge = lane == 0
        return jnp.concatenate([jnp.where(edge, halo, lo), jnp.where(edge, lo, hi)], 1)

    def mirrored(q):
        return [q[0], q[1], -q[2], q[3], q[4], q[5]]

    got = [swapped[v, radial:] for v in range(6)]
    bottom = [prim[v, :, 0, :] for v in range(6)]
    ceiling = [prim[v, :, radial - 1, :] for v in range(6)]
    high = [jnp.where(at_low, g, w) for g, w in zip(got, mirrored(ceiling))]
    low = [jnp.where(at_low, w, g) for g, w in zip(got, mirrored(bottom))]
    high_state = pack_state(state_of(high))
    for i, name in enumerate(PASSED):
        lay_hi[i] = high_state[name]
    for i, f in enumerate(face_of(state_of(low), state_of(bottom), 1)):
        lay_lo[i] = f
    for i in range(3):
        lay_u[i] = low[1 + i]

    def column(ref, v):
        q = ref[v, :, ref.shape[2] - LANES :]
        return jnp.where(lane < count, q, 1.0)

    nxt_state = pack_state(state_of([column(col_next, v) for v in range(6)]))
    for i, name in enumerate(PASSED):
        azi_hi[i] = nxt_state[name]
    prev = [column(came, v) for v in range(6)]
    for i, f in enumerate(face_of(state_of(prev), state_of([column(col_own, v) for v in range(6)]), 2)):
        azi_lo[i] = f
    for i in range(3):
        azi_u[i] = prev[1 + i]

    end = [core[v] for v in range(6)]
    end_state = state_of(end)
    no_low = jnp.where(even, 0.0, 1.0)
    no_high = jnp.where(even, 1.0, 0.0)
    for i, f in enumerate(face_of(end_state, state_at(prim, der, 0), 0)):
        low_face[i] = f * no_low

    def step(a, _):
        here = state_at(prim, der, a)
        last = a == count - 1
        first = a == 0
        later = jnp.minimum(a + 1, count - 1)
        earlier = jnp.maximum(a - 1, 0)
        total = [None] * 6
        above = state_at(prim, der, later)
        right = dict(
            (k, [jnp.where(last, g, h) for g, h in zip(end_state[k], above[k])])
            if isinstance(above[k], list)
            else (k, jnp.where(last, end_state[k], above[k]))
            for k in above
        )
        keep = jnp.where(last, no_high, 1.0)
        for i, f in enumerate(face_of(here, right, 0)):
            f = f * keep
            total[i] = f - low_face[i]
            low_face[i] = f
        grad2 = None
        for i in range(3):
            down = jnp.where(first, end[1 + i], prim[1 + i, earlier])
            d = right["u"][i] - down
            grad2 = d * d if grad2 is None else grad2 + d * d
        outermost = jnp.where(even, first, last)
        grad2 = grad2 * jnp.where(outermost, 0.0, 1.0)
        packed = pack_state(here)
        row_of = pl.ds(a, 1)
        shifted = {n: up_r(packed[n], lay_hi[i, row_of, :]) for i, n in enumerate(PASSED)}
        face = face_of(here, unpack_state(shifted), 1)
        for i, f in enumerate(face):
            total[i] = total[i] + (f - down_r(f, lay_lo[i, row_of, :]))
        for i in range(3):
            d = shifted["u%d" % i] - down_r(here["u"][i], lay_u[i, row_of, :])
            grad2 = grad2 + d * d
        to_end = (LANES - 1) - a
        to_start = (LANES - a) % LANES
        shifted = {n: up_t(packed[n], pltpu.roll(azi_hi[i], to_end, 1)) for i, n in enumerate(PASSED)}
        face = face_of(here, unpack_state(shifted), 2)
        for i, f in enumerate(face):
            total[i] = total[i] + (f - down_t(f, pltpu.roll(azi_lo[i], to_start, 1)))
        for i in range(3):
            d = shifted["u%d" % i] - down_t(here["u"][i], pltpu.roll(azi_u[i], to_start, 1))
            grad2 = grad2 + d * d
        shielding, source = closure(here["rho"], prim[5, a], wall[a], grad2)
        for i in range(6):
            total_out[i, a] = total[i]
        shield[a] = shielding
        source_out[a] = source

        @pl.when(outermost)
        def _():
            grad_out[...] = grad2

        return 0

    lax.fori_loop(0, count, step, 0)


def finish_kernel(
    prim, der, wall, total, shield, source, grad, sent, ghost, top,
    flow_out, shield_out, flow, edge_flow, edge_shield, sems,
):
    _, count, radial, width = prim.shape
    row = lax.axis_index("row")
    even = row % 2 == 0
    coupled = (row == 1) | (row == 2)
    step_size = CFL / jnp.max(top[...])
    half = 0.5 * step_size

    edge = jnp.where(even, 0, count - 1)
    inside = jnp.where(even, 1, count - 2)
    here = state_at(prim, der, edge)
    beyond = [jnp.where(coupled, ghost[v], sent[v, :, :width]) for v in range(6)]
    out_state = state_of(beyond)
    grad2 = grad[...]
    for i in range(3):
        d = prim[1 + i, inside] - beyond[1 + i]
        grad2 = grad2 + d * d

    def pick(p, q):
        return dict(
            (k, [jnp.where(even, x, y) for x, y in zip(p[k], q[k])])
            if isinstance(p[k], list)
            else (k, jnp.where(even, p[k], q[k]))
            for k in p
        )

    sign = jnp.where(even, -1.0, 1.0)
    shielding, fixed = closure(here["rho"], prim[5, edge], wall[edge], grad2)
    edge_shield[...] = shielding
    copies = [
        pltpu.make_async_copy(edge_shield, shield_out.at[edge], sems.at[0]),
        pltpu.make_async_copy(
            shield.at[pl.ds(1 - edge // (count - 1), count - 1)],
            shield_out.at[pl.ds(1 - edge // (count - 1), count - 1)],
            sems.at[1],
        ),
    ]
    for copy in copies:
        copy.start()
    cons = cons_of(here)
    for i, f in enumerate(face_of(pick(out_state, here), pick(here, out_state), 0)):
        value = cons[i] - half * (total[i, edge] + sign * f)
        edge_flow[i] = value + step_size * fixed if i == 5 else value
    chunk = 4
    for k in range(count // chunk):

        def step(j, _):
            a = k * chunk + j
            flow[0, a] = prim[0, a] - half * total[0, a]
            for i in range(4):
                flow[1 + i, a] = der[i, a] - half * total[1 + i, a]
            flow[5, a] = der[4, a] - half * total[5, a] + step_size * source[a]
            return 0

        lax.fori_loop(0, chunk, step, 0)

        @pl.when(edge // chunk == k)
        def _():
            for i in range(6):
                flow[i, edge] = edge_flow[i]

        rows = pl.ds(k * chunk, chunk)
        copy = pltpu.make_async_copy(flow.at[:, rows], flow_out.at[:, rows], sems.at[2 + k])
        copy.start()
        copies.append(copy)
    for copy in copies:
        copy.wait()


def body(density, velocity, pressure, nu_tilde, wall_distance, interp_fwd, interp_back, offset):
    rows, rads, cycle = (lax.axis_size(n) for n in AXES)
    count, radial, width = density.shape
    devices = rows * rads * cycle

    def device(row, rad, azi):
        return (row * rads + rad) * cycle + azi % cycle

    def everyone(target):
        return [
            (device(r, d, a), target(r, d, a))
            for r in range(rows)
            for d in range(rads)
            for a in range(cycle)
        ]

    plane = shaped(6, radial, width)
    block = shaped(count, radial, width)
    six = shaped(6, count, radial, width)
    prim, der, wall, core, up_send, layer, col_down, top = pl.pallas_call(
        derive_kernel,
        out_shape=(
            six, six, block, plane, shaped(6, radial, width + LANES), shaped(6, count, width),
            shaped(6, radial, LANES), shaped(devices, 1, LANES),
        ),
        in_specs=[HBM] * 5,
        out_specs=(VMEM,) * 8,
        scratch_shapes=[pltpu.SemaphoreType.DMA((5,))],
        compiler_params=params(),
        name="derive",
    )(density, velocity, pressure, nu_tilde, wall_distance)

    up = everyone(lambda r, d, a: device(r, d, a + 1))
    down = everyone(lambda r, d, a: device(r, d, a - 1))
    pair = everyone(lambda r, d, a: device(r ^ 1, d, a))
    across = everyone(lambda r, d, a: device(r, rads - 1 - d, a))
    tops = lax.all_to_all(top, AXES, 0, 0)
    came = lax.ppermute(up_send, AXES, up)
    col_next = lax.ppermute(col_down, AXES, down)
    core_got = lax.ppermute(core, AXES, pair)

    moved = pl.pallas_call(
        shift_kernel,
        out_shape=shaped(6, radial + count, width),
        in_specs=[SMEM, VMEM, VMEM, VMEM],
        out_specs=VMEM,
        compiler_params=params(),
        name="shift",
    )(offset, came, up_send, layer)
    swapped = lax.ppermute(moved, AXES, across)
    weighted = pl.pallas_call(
        weight_kernel,
        out_shape=plane,
        in_specs=[VMEM] * 4,
        out_specs=VMEM,
        compiler_params=params(),
        name="weigh",
    )(interp_fwd, interp_back, moved, swapped)

    faces = pl.pallas_call(
        face_kernel,
        out_shape=(six, block, block, shaped(radial, width)),
        in_specs=[VMEM] * 8,
        out_specs=(VMEM,) * 4,
        scratch_shapes=[
            pltpu.VMEM((6, radial, width), F32),
            pltpu.VMEM((8, count, width), F32),
            pltpu.VMEM((6, count, width), F32),
            pltpu.VMEM((3, count, width), F32),
            pltpu.VMEM((8, radial, LANES), F32),
            pltpu.VMEM((6, radial, LANES), F32),
            pltpu.VMEM((3, radial, LANES), F32),
        ],
        compiler_params=params(),
        cost_estimate=pl.CostEstimate(flops=25_000_000, bytes_accessed=6_000_000, transcendentals=300_000),
        name="faces",
    )

    def far(blocks):
        route = []
        for d in range(rads):
            for a in range(cycle):
                route.append((device(1, d, a), device(2, d, a + blocks)))
                route.append((device(2, d, a), device(1, d, a + cycle - 1 - blocks)))

        def branch(block, *rest):
            return lax.ppermute(block, AXES, route), faces(*rest)

        return branch

    ghost, (total, shield, source, grad) = lax.switch(
        offset[0] // width,
        [far(b) for b in range(cycle)],
        weighted, prim, der, wall, core_got, swapped, came, col_next, col_down,
    )

    return pl.pallas_call(
        finish_kernel,
        out_shape=(six, block),
        in_specs=[VMEM] * 10,
        out_specs=(HBM, HBM),
        scratch_shapes=[
            pltpu.VMEM((6, count, radial, width), F32),
            pltpu.VMEM((6, radial, width), F32),
            pltpu.VMEM((radial, width), F32),
            pltpu.SemaphoreType.DMA((2 + count // 4,)),
        ],
        compiler_params=params(),
        name="finish",
    )(prim, der, wall, total, shield, source, grad, up_send, ghost, tops)


def solution(mesh):
    placed = (
        P("row", "rad", "azi"),
        P(None, "row", "rad", "azi"),
        P("row", "rad", "azi"),
        P("row", "rad", "azi"),
        P("row", "rad", "azi"),
        P("rad", None),
        P("rad", None),
        P(),
    )
    return jax.shard_map(
        body,
        mesh=mesh,
        in_specs=placed,
        out_specs=(P(None, "row", "rad", "azi"), P("row", "rad", "azi")),
        check_vma=False,
    )
```

```python
import functools

import jax
import jax.numpy as jnp
from jax import lax
from jax.experimental import pallas as pl
from jax.experimental.pallas import tpu as pltpu
from jax.sharding import PartitionSpec as P

GAMMA = 1.4
CFL = 0.8
KAPPA = 0.41
C_DES = 0.65
CB1 = 0.1355
CW1 = 3.239
NU_LAM = 0.001
GRAD_FLOOR = 0.2

AXES = ("row", "rad", "azi")
LANES = 128
CHUNK = 4
F32 = jnp.float32
VMEM = pl.BlockSpec(memory_space=pltpu.VMEM)
SMEM = pl.BlockSpec(memory_space=pltpu.SMEM)
HBM = pl.BlockSpec(memory_space=pltpu.HBM)


def params(mib=32):
    return pltpu.CompilerParams(vmem_limit_bytes=mib * 1024 * 1024)


def shaped(*dims):
    return jax.ShapeDtypeStruct(dims, F32)


def apart(*dims):
    return pltpu.HBM(dims, F32)


def far_away(array):
    return pltpu.with_memory_space_constraint(array, pltpu.HBM)


def sound_speed(rho, press):
    return jnp.sqrt(GAMMA * press / rho)


def energy_of(press, m, u):
    return press * (1.0 / (GAMMA - 1.0)) + 0.5 * (m[0] * u[0] + m[1] * u[1] + m[2] * u[2])


def state_of(prim):
    rho, u, press, nut = prim[0], prim[1:4], prim[4], prim[5]
    m = [rho * v for v in u]
    return dict(
        rho=rho, m=m, u=u, p=press, e=energy_of(press, m, u), n=rho * nut, c=sound_speed(rho, press)
    )


def cons_of(s):
    return [s["rho"], s["m"][0], s["m"][1], s["m"][2], s["e"], s["n"]]


def flux_of(s, k):
    w = s["u"][k]
    mom = [s["m"][k] * s["u"][i] for i in range(3)]
    mom[k] = mom[k] + s["p"]
    return [s["m"][k], mom[0], mom[1], mom[2], (s["e"] + s["p"]) * w, s["n"] * w]


def face_of(left, right, k):
    wave = jnp.maximum(jnp.abs(left["u"][k]) + left["c"], jnp.abs(right["u"][k]) + right["c"])
    return [
        (fl + fr) - wave * (ur - ul)
        for fl, fr, ul, ur in zip(
            flux_of(left, k), flux_of(right, k), cons_of(left), cons_of(right)
        )
    ]


NAMES = ("rho", "u0", "u1", "u2", "p", "m0", "m1", "m2", "e", "n", "c")
PASSED = ("rho", "u0", "u1", "u2", "p", "e", "n", "c")


def pack_state(s):
    return dict(
        rho=s["rho"], u0=s["u"][0], u1=s["u"][1], u2=s["u"][2], p=s["p"], e=s["e"], n=s["n"], c=s["c"]
    )


def unpack_state(d):
    u = [d["u0"], d["u1"], d["u2"]]
    return dict(rho=d["rho"], u=u, m=[d["rho"] * v for v in u], p=d["p"], e=d["e"], n=d["n"], c=d["c"])


def fetch(sources, prim, rows, sems):
    rho, vel, press, nut = sources
    return [
        pltpu.make_async_copy(rho.at[rows], prim.at[0, rows], sems.at[0]),
        pltpu.make_async_copy(vel.at[:, rows], prim.at[pl.ds(1, 3), rows], sems.at[1]),
        pltpu.make_async_copy(press.at[rows], prim.at[4, rows], sems.at[2]),
        pltpu.make_async_copy(nut.at[rows], prim.at[5, rows], sems.at[3]),
    ]


def derive_kernel(
    rho_in, vel_in, press_in, nut_in, core, up_send, layer, far_layer, col_down, top, prim, sems,
):
    _, count, radial, width = prim.shape
    even = lax.axis_index("row") % 2 == 0
    inner_rad = lax.axis_index("rad") == 0
    lane = lax.broadcasted_iota(jnp.int32, (radial, LANES), 1)
    parts = count // CHUNK

    def part_of(k):
        return fetch((rho_in, vel_in, press_in, nut_in), prim, pl.ds(k * CHUNK, CHUNK), sems.at[k])

    for k in range(parts):
        for c in part_of(k):
            c.start()
    up_send[:, :, width:] = jnp.zeros((6, radial, LANES), F32)
    col_down[...] = jnp.zeros(col_down.shape, F32)

    def step(a, best):
        speed = 3.0 * sound_speed(prim[0, a], prim[4, a])
        here = lane == a
        for v in range(6):
            plane = prim[v, a]
            if 1 <= v <= 3:
                speed = speed + jnp.abs(plane)
            high, low = plane[radial - 1 :], plane[:1]
            layer[v, pl.ds(a, 1), :] = jnp.where(inner_rad, high, low)
            far_layer[v, pl.ds(a, 1), :] = jnp.where(inner_rad, low, high)
            first, last = plane[:, :LANES], plane[:, width - LANES :]
            up_send[v, :, width:] = jnp.where(
                here, pltpu.roll(last, a + 1, 1), up_send[v, :, width:]
            )
            col_down[v] = jnp.where(here, pltpu.roll(first, a, 1), col_down[v])
        return jnp.maximum(best, speed)

    def part_step(k, best):
        for c in part_of(k):
            c.wait()
        return lax.fori_loop(k * CHUNK, (k + 1) * CHUNK, step, best)

    best = lax.fori_loop(0, parts, part_step, jnp.zeros((radial, width), F32))
    largest = jnp.max(best, axis=0, keepdims=True)
    largest = jnp.max(largest, axis=1, keepdims=True)
    for v in range(6):
        low, high = prim[v, 0], prim[v, count - 1]
        core[v] = jnp.where(even, high, low)
        up_send[v, :, :width] = jnp.where(even, low, high)
    top[...] = jnp.broadcast_to(largest.reshape(1, 1, 1), top.shape)


def shift_kernel(shift, came, sent, out):
    radial, width = out.shape[1], out.shape[2]
    row = lax.axis_index("row")
    amount = shift[0] % width
    amount = jnp.where(row == 1, amount, jnp.where(row == 2, width - amount, 0))
    tiles = amount // LANES
    rest = amount % LANES
    lane = lax.broadcasted_iota(jnp.int32, (radial, LANES), 1)
    for v in range(6):
        parts = [
            pltpu.roll(ref[v, :, h * LANES : (h + 1) * LANES], rest, 1)
            for ref in (came, sent)
            for h in range(2)
        ]
        for t in range(2):
            picks = [
                jnp.where(lane < rest, parts[max(1 + t - q, 0)], parts[2 + t - q]) for q in range(3)
            ]
            out[v, :, t * LANES : (t + 1) * LANES] = jnp.where(
                tiles == 0, picks[0], jnp.where(tiles == 1, picks[1], picks[2])
            )


def weight_kernel(fwd, back, own, other, out):
    radial = out.shape[1]
    low = lax.axis_index("rad") == 0
    table = jnp.where(lax.axis_index("row") == 1, fwd[...], back[...])
    for v in range(6):
        mine, theirs = own[v], other[v]
        plane = jnp.concatenate([jnp.where(low, mine, theirs), jnp.where(low, theirs, mine)], 0)
        out[v] = jnp.dot(
            table, plane, precision=lax.Precision.HIGHEST, preferred_element_type=F32
        )


def closure(rho, nut, dist, grad2):
    strain = jnp.maximum(jnp.sqrt(0.25 * grad2), GRAD_FLOOR)
    ratio = (nut + NU_LAM) / (KAPPA * KAPPA * dist * dist * strain)
    eight = 8.0 * ratio
    shielding = 1.0 - jnp.tanh(eight * eight * eight)
    length = dist - shielding * jnp.maximum(0.0, dist - C_DES)
    quot = nut / length
    return shielding, rho * (CB1 * strain * nut - CW1 * (quot * quot))


def state_at(prim, der, a):
    return dict(
        rho=prim[0, a],
        u=[prim[1 + i, a] for i in range(3)],
        p=prim[4, a],
        m=[der[i, a] for i in range(3)],
        e=der[3, a],
        n=der[4, a],
        c=der[5, a],
    )


def face_kernel(
    rho_in, vel_in, press_in, nut_in, wall_in, core, layer, own_layer, wall_layer, came, col_next,
    col_own, top, flow_out, shield_out, edge_out,
    prim, der, wall, flow, shield,
    low_face, lay_hi, lay_lo, lay_u, azi_hi, azi_lo, azi_u, sems, out_sems,
):
    _, count, radial, width = prim.shape
    row, rad = lax.axis_index("row"), lax.axis_index("rad")
    even = row % 2 == 0
    at_low = rad == 0
    parts = count // CHUNK

    def part_of(k):
        rows = pl.ds(k * CHUNK, CHUNK)
        part = fetch((rho_in, vel_in, press_in, nut_in), prim, rows, sems.at[k])
        return part + [pltpu.make_async_copy(wall_in.at[rows], wall.at[rows], sems.at[k, 4])]

    def results_of(k):
        rows = pl.ds(k * CHUNK, CHUNK)
        return [
            pltpu.make_async_copy(flow.at[:, rows], flow_out.at[:, rows], out_sems.at[k, 0]),
            pltpu.make_async_copy(shield.at[rows], shield_out.at[rows], out_sems.at[k, 1]),
        ]

    for k in range(parts):
        for c in part_of(k):
            c.start()
    step_size = CFL / jnp.max(top[...])
    half = 0.5 * step_size
    sub = lax.broadcasted_iota(jnp.int32, (8, width), 0)
    lane = lax.broadcasted_iota(jnp.int32, (radial, LANES), 1)

    def derive(a):
        q = [prim[v, a] for v in range(6)]
        s = state_of(q)
        for i in range(3):
            der[i, a] = s["m"][i]
        der[3, a] = s["e"]
        der[4, a] = s["n"]
        der[5, a] = s["c"]

    def up_r(v, halo):
        lo, hi = pltpu.roll(v[:8], 7, 0), pltpu.roll(v[8:], 7, 0)
        edge = sub == 7
        return jnp.concatenate([jnp.where(edge, hi, lo), jnp.where(edge, halo, hi)], 0)

    def down_r(v, halo):
        lo, hi = pltpu.roll(v[:8], 1, 0), pltpu.roll(v[8:], 1, 0)
        edge = sub == 0
        return jnp.concatenate([jnp.where(edge, halo, lo), jnp.where(edge, lo, hi)], 0)

    def up_t(v, halo):
        lo, hi = pltpu.roll(v[:, :LANES], LANES - 1, 1), pltpu.roll(v[:, LANES:], LANES - 1, 1)
        edge = lane == LANES - 1
        return jnp.concatenate([jnp.where(edge, hi, lo), jnp.where(edge, halo, hi)], 1)

    def down_t(v, halo):
        lo, hi = pltpu.roll(v[:, :LANES], 1, 1), pltpu.roll(v[:, LANES:], 1, 1)
        edge = lane == 0
        return jnp.concatenate([jnp.where(edge, halo, lo), jnp.where(edge, lo, hi)], 1)

    def mirrored(q):
        return [q[0], q[1], -q[2], q[3], q[4], q[5]]

    got = [layer[v] for v in range(6)]
    bottom = [jnp.where(at_low, wall_layer[v], own_layer[v]) for v in range(6)]
    ceiling = [jnp.where(at_low, own_layer[v], wall_layer[v]) for v in range(6)]
    high = [jnp.where(at_low, g, w) for g, w in zip(got, mirrored(ceiling))]
    low = [jnp.where(at_low, w, g) for g, w in zip(got, mirrored(bottom))]
    high_state = pack_state(state_of(high))
    for i, name in enumerate(PASSED):
        lay_hi[i] = high_state[name]
    for i, f in enumerate(face_of(state_of(low), state_of(bottom), 1)):
        lay_lo[i] = f
    for i in range(3):
        lay_u[i] = low[1 + i]

    def column(ref, v):
        q = ref[v, :, ref.shape[2] - LANES :]
        return jnp.where(lane < count, q, 1.0)

    nxt_state = pack_state(state_of([column(col_next, v) for v in range(6)]))
    for i, name in enumerate(PASSED):
        azi_hi[i] = nxt_state[name]
    prev = [column(came, v) for v in range(6)]
    for i, f in enumerate(face_of(state_of(prev), state_of([column(col_own, v) for v in range(6)]), 2)):
        azi_lo[i] = f
    for i in range(3):
        azi_u[i] = prev[1 + i]

    end = [core[v] for v in range(6)]
    end_state = state_of(end)
    no_low = jnp.where(even, 0.0, 1.0)
    no_high = jnp.where(even, 1.0, 0.0)
    for c in part_of(0):
        c.wait()
    derive(0)
    for i, f in enumerate(face_of(end_state, state_at(prim, der, 0), 0)):
        low_face[i] = f * no_low

    def step(a, _):
        here = state_at(prim, der, a)
        last = a == count - 1
        first = a == 0
        later = jnp.minimum(a + 1, count - 1)
        earlier = jnp.maximum(a - 1, 0)
        total = [None] * 6
        derive(later)
        above = state_at(prim, der, later)
        right = dict(
            (k, [jnp.where(last, g, h) for g, h in zip(end_state[k], above[k])])
            if isinstance(above[k], list)
            else (k, jnp.where(last, end_state[k], above[k]))
            for k in above
        )
        keep = jnp.where(last, no_high, 1.0)
        for i, f in enumerate(face_of(here, right, 0)):
            f = f * keep
            total[i] = f - low_face[i]
            low_face[i] = f
        grad2 = None
        for i in range(3):
            down = jnp.where(first, end[1 + i], prim[1 + i, earlier])
            d = right["u"][i] - down
            grad2 = d * d if grad2 is None else grad2 + d * d
        outermost = jnp.where(even, first, last)
        grad2 = grad2 * jnp.where(outermost, 0.0, 1.0)
        packed = pack_state(here)
        row_of = pl.ds(a, 1)
        shifted = {n: up_r(packed[n], lay_hi[i, row_of, :]) for i, n in enumerate(PASSED)}
        face = face_of(here, unpack_state(shifted), 1)
        for i, f in enumerate(face):
            total[i] = total[i] + (f - down_r(f, lay_lo[i, row_of, :]))
        for i in range(3):
            d = shifted["u%d" % i] - down_r(here["u"][i], lay_u[i, row_of, :])
            grad2 = grad2 + d * d
        to_end = (LANES - 1) - a
        to_start = (LANES - a) % LANES
        shifted = {n: up_t(packed[n], pltpu.roll(azi_hi[i], to_end, 1)) for i, n in enumerate(PASSED)}
        face = face_of(here, unpack_state(shifted), 2)
        for i, f in enumerate(face):
            total[i] = total[i] + (f - down_t(f, pltpu.roll(azi_lo[i], to_start, 1)))
        for i in range(3):
            d = shifted["u%d" % i] - down_t(here["u"][i], pltpu.roll(azi_u[i], to_start, 1))
            grad2 = grad2 + d * d
        shielding, source = closure(here["rho"], prim[5, a], wall[a], grad2)
        cons = cons_of(here)
        for i in range(5):
            flow[i, a] = cons[i] - half * total[i]
        flow[5, a] = cons[5] - half * total[5] + step_size * source
        shield[a] = shielding

        @pl.when(outermost)
        def _():
            for i in range(6):
                edge_out[i] = cons[i] - half * total[i]
            edge_out[6] = grad2
            edge_out[7] = wall[a]
            inside = jnp.where(even, 1, count - 2)
            for i in range(3):
                edge_out[8 + i] = prim[1 + i, inside]
            edge_out[11] = jnp.zeros((radial, width), F32) + step_size

        return 0

    def part_step(k, _):
        @pl.when(k + 1 < parts)
        def _():
            for c in part_of(k + 1):
                c.wait()

        lax.fori_loop(k * CHUNK, (k + 1) * CHUNK, step, 0)
        for c in results_of(k):
            c.start()
        return 0

    lax.fori_loop(0, parts, part_step, 0)
    for k in range(parts):
        for c in results_of(k):
            c.wait()


def edge_kernel(
    flow_in, shield_in, edge, sent, ghost, flow_out, shield_out, edge_flow, edge_shield, sems
):
    del flow_in, shield_in
    _, radial, width = ghost.shape
    count = shield_out.shape[0]
    row = lax.axis_index("row")
    even = row % 2 == 0
    coupled = (row == 1) | (row == 2)
    step_size = edge[11]
    end = jnp.where(even, 0, count - 1)
    mine = [sent[v, :, :width] for v in range(6)]
    beyond = [jnp.where(coupled, ghost[v], mine[v]) for v in range(6)]
    here, out_state = state_of(mine), state_of(beyond)
    grad2 = edge[6]
    for i in range(3):
        d = edge[8 + i] - beyond[1 + i]
        grad2 = grad2 + d * d

    def pick(p, q):
        return dict(
            (k, [jnp.where(even, x, y) for x, y in zip(p[k], q[k])])
            if isinstance(p[k], list)
            else (k, jnp.where(even, p[k], q[k]))
            for k in p
        )

    shielding, source = closure(here["rho"], mine[5], edge[7], grad2)
    edge_shield[...] = shielding
    sign = jnp.where(even, -0.5, 0.5)
    for i, f in enumerate(face_of(pick(out_state, here), pick(here, out_state), 0)):
        value = edge[i] - step_size * (sign * f)
        edge_flow[i] = value + step_size * source if i == 5 else value
    copies = [
        pltpu.make_async_copy(edge_flow, flow_out.at[:, end], sems.at[0]),
        pltpu.make_async_copy(edge_shield, shield_out.at[end], sems.at[1]),
    ]
    for c in copies:
        c.start()
    for c in copies:
        c.wait()


def body(density, velocity, pressure, nu_tilde, wall_distance, interp_fwd, interp_back, offset):
    rows, rads, cycle = (lax.axis_size(n) for n in AXES)
    count, radial, width = density.shape

    def device(row, rad, azi):
        return (row * rads + rad) * cycle + azi % cycle

    def everyone(target):
        return [
            (device(r, d, a), target(r, d, a))
            for r in range(rows)
            for d in range(rads)
            for a in range(cycle)
        ]

    plane = shaped(6, radial, width)
    wide = shaped(6, radial, width + LANES)
    column = shaped(6, radial, LANES)
    devices = rows * rads * cycle
    whole = (6, count, radial, width)
    parts = count // CHUNK
    fields = [far_away(x) for x in (density, velocity, pressure, nu_tilde)]
    dma = pltpu.SemaphoreType.DMA
    core, up_send, layer, far_layer, col_down, top = pl.pallas_call(
        derive_kernel,
        out_shape=(
            plane, wide, shaped(6, count, width), shaped(6, count, width), column,
            shaped(devices, 1, LANES),
        ),
        in_specs=[HBM] * 4,
        out_specs=(VMEM,) * 6,
        scratch_shapes=[pltpu.VMEM(whole, F32), dma((parts, 4))],
        compiler_params=params(),
        name="derive",
    )(*fields)

    up = everyone(lambda r, d, a: device(r, d, a + 1))
    down = everyone(lambda r, d, a: device(r, d, a - 1))
    pair = everyone(lambda r, d, a: device(r ^ 1, d, a))
    across = everyone(lambda r, d, a: device(r, rads - 1 - d, a))
    tops = lax.all_to_all(top, AXES, 0, 0)
    came = lax.ppermute(up_send, AXES, up)
    col_next = lax.ppermute(col_down, AXES, down)
    core_got = lax.ppermute(core, AXES, pair)

    moved = pl.pallas_call(
        shift_kernel,
        out_shape=plane,
        in_specs=[SMEM, VMEM, VMEM],
        out_specs=VMEM,
        compiler_params=params(),
        name="shift",
    )(offset, came, up_send)
    swapped = lax.ppermute(moved, AXES, across)
    swapped, layer = lax.optimization_barrier((swapped, layer))
    layer_got = lax.ppermute(layer, AXES, across)
    weighted = pl.pallas_call(
        weight_kernel,
        out_shape=plane,
        in_specs=[VMEM] * 4,
        out_specs=VMEM,
        compiler_params=params(),
        name="weigh",
    )(interp_fwd, interp_back, moved, swapped)

    faces = pl.pallas_call(
        face_kernel,
        out_shape=(apart(*whole), apart(count, radial, width), shaped(12, radial, width)),
        in_specs=[HBM] * 5 + [VMEM] * 8,
        out_specs=(HBM, HBM, VMEM),
        scratch_shapes=[
            pltpu.VMEM(whole, F32),
            pltpu.VMEM(whole, F32),
            pltpu.VMEM((count, radial, width), F32),
            pltpu.VMEM(whole, F32),
            pltpu.VMEM((count, radial, width), F32),
            pltpu.VMEM((6, radial, width), F32),
            pltpu.VMEM((8, count, width), F32),
            pltpu.VMEM((6, count, width), F32),
            pltpu.VMEM((3, count, width), F32),
            pltpu.VMEM((8, radial, LANES), F32),
            pltpu.VMEM((6, radial, LANES), F32),
            pltpu.VMEM((3, radial, LANES), F32),
            dma((parts, 5)),
            dma((parts, 2)),
        ],
        compiler_params=params(),
        cost_estimate=pl.CostEstimate(
            flops=25_000_000, bytes_accessed=6_000_000, transcendentals=300_000
        ),
        name="faces",
    )

    def far(blocks):
        route = []
        for d in range(rads):
            for a in range(cycle):
                route.append((device(1, d, a), device(2, d, a + blocks)))
                route.append((device(2, d, a), device(1, d, a + cycle - 1 - blocks)))

        def branch(block, arrays, *rest):
            return lax.ppermute(block, AXES, route), faces(*map(far_away, arrays), *rest)

        return branch

    ghost, (flow, shield, edge) = lax.switch(
        offset[0] // width,
        [far(b) for b in range(cycle)],
        weighted, (density, velocity, pressure, nu_tilde, wall_distance),
        core_got, layer_got, layer, far_layer, came, col_next, col_down, tops,
    )

    return pl.pallas_call(
        edge_kernel,
        out_shape=(shaped(*whole), shaped(count, radial, width)),
        in_specs=[HBM] * 2 + [VMEM] * 3,
        out_specs=(HBM, HBM),
        input_output_aliases={0: 0, 1: 1},
        scratch_shapes=[
            pltpu.VMEM((6, radial, width), F32),
            pltpu.VMEM((radial, width), F32),
            dma((2,)),
        ],
        compiler_params=params(),
        name="edge",
    )(far_away(flow), far_away(shield), edge, up_send, ghost)


def solution(mesh):
    placed = (
        P("row", "rad", "azi"),
        P(None, "row", "rad", "azi"),
        P("row", "rad", "azi"),
        P("row", "rad", "azi"),
        P("row", "rad", "azi"),
        P("rad", None),
        P("rad", None),
        P(),
    )
    return jax.shard_map(
        body,
        mesh=mesh,
        in_specs=placed,
        out_specs=(P(None, "row", "rad", "azi"), P("row", "rad", "azi")),
        check_vma=False,
    )
```

```python
import functools

import jax
import jax.numpy as jnp
from jax import lax
from jax.experimental import pallas as pl
from jax.experimental.pallas import tpu as pltpu
from jax.sharding import PartitionSpec as P

GAMMA = 1.4
CFL = 0.8
KAPPA = 0.41
C_DES = 0.65
CB1 = 0.1355
CW1 = 3.239
NU_LAM = 0.001
GRAD_FLOOR = 0.2

AXES = ("row", "rad", "azi")
LANES = 128
CHUNK = 4
F32 = jnp.float32
VMEM = pl.BlockSpec(memory_space=pltpu.VMEM)
SMEM = pl.BlockSpec(memory_space=pltpu.SMEM)
HBM = pl.BlockSpec(memory_space=pltpu.HBM)


def params(mib=32):
    return pltpu.CompilerParams(vmem_limit_bytes=mib * 1024 * 1024)


def shaped(*dims):
    return jax.ShapeDtypeStruct(dims, F32)


def apart(*dims):
    return pltpu.HBM(dims, F32)


def far_away(array):
    return pltpu.with_memory_space_constraint(array, pltpu.HBM)


def sound_speed(rho, press):
    return jnp.sqrt(GAMMA * press / rho)


def energy_of(press, m, u):
    return press * (1.0 / (GAMMA - 1.0)) + 0.5 * (m[0] * u[0] + m[1] * u[1] + m[2] * u[2])


def state_of(prim):
    rho, u, press, nut = prim[0], prim[1:4], prim[4], prim[5]
    m = [rho * v for v in u]
    return dict(
        rho=rho, m=m, u=u, p=press, e=energy_of(press, m, u), n=rho * nut, c=sound_speed(rho, press)
    )


def cons_of(s):
    return [s["rho"], s["m"][0], s["m"][1], s["m"][2], s["e"], s["n"]]


def flux_of(s, k):
    w = s["u"][k]
    mom = [s["m"][k] * s["u"][i] for i in range(3)]
    mom[k] = mom[k] + s["p"]
    return [s["m"][k], mom[0], mom[1], mom[2], (s["e"] + s["p"]) * w, s["n"] * w]


def face_of(left, right, k):
    wave = jnp.maximum(jnp.abs(left["u"][k]) + left["c"], jnp.abs(right["u"][k]) + right["c"])
    return [
        (fl + fr) - wave * (ur - ul)
        for fl, fr, ul, ur in zip(
            flux_of(left, k), flux_of(right, k), cons_of(left), cons_of(right)
        )
    ]


NAMES = ("rho", "u0", "u1", "u2", "p", "m0", "m1", "m2", "e", "n", "c")
PASSED = ("rho", "u0", "u1", "u2", "p", "e", "n", "c")


def pack_state(s):
    return dict(
        rho=s["rho"], u0=s["u"][0], u1=s["u"][1], u2=s["u"][2], p=s["p"], e=s["e"], n=s["n"], c=s["c"]
    )


def unpack_state(d):
    u = [d["u0"], d["u1"], d["u2"]]
    return dict(rho=d["rho"], u=u, m=[d["rho"] * v for v in u], p=d["p"], e=d["e"], n=d["n"], c=d["c"])


def fetch(sources, prim, rows, sems):
    rho, vel, press, nut = sources
    return [
        pltpu.make_async_copy(rho.at[rows], prim.at[0, rows], sems.at[0]),
        pltpu.make_async_copy(vel.at[:, rows], prim.at[pl.ds(1, 3), rows], sems.at[1]),
        pltpu.make_async_copy(press.at[rows], prim.at[4, rows], sems.at[2]),
        pltpu.make_async_copy(nut.at[rows], prim.at[5, rows], sems.at[3]),
    ]


def derive_kernel(
    rho_in, vel_in, press_in, nut_in, core, up_send, layer, far_layer, col_down, top, prim, sems,
):
    _, count, radial, width = prim.shape
    even = lax.axis_index("row") % 2 == 0
    inner_rad = lax.axis_index("rad") == 0
    lane = lax.broadcasted_iota(jnp.int32, (radial, LANES), 1)
    parts = count // CHUNK

    def part_of(k):
        return fetch((rho_in, vel_in, press_in, nut_in), prim, pl.ds(k * CHUNK, CHUNK), sems.at[k])

    for k in range(parts):
        for c in part_of(k):
            c.start()
    up_send[:, :, width:] = jnp.zeros((6, radial, LANES), F32)
    col_down[...] = jnp.zeros(col_down.shape, F32)

    def step(a, best):
        speed = 3.0 * sound_speed(prim[0, a], prim[4, a])
        here = lane == a
        for v in range(6):
            plane = prim[v, a]
            if 1 <= v <= 3:
                speed = speed + jnp.abs(plane)
            high, low = plane[radial - 1 :], plane[:1]
            layer[v, pl.ds(a, 1), :] = jnp.where(inner_rad, high, low)
            far_layer[v, pl.ds(a, 1), :] = jnp.where(inner_rad, low, high)
            first, last = plane[:, :LANES], plane[:, width - LANES :]
            up_send[v, :, width:] = jnp.where(
                here, pltpu.roll(last, a + 1, 1), up_send[v, :, width:]
            )
            col_down[v] = jnp.where(here, pltpu.roll(first, a, 1), col_down[v])
        return jnp.maximum(best, speed)

    best = jnp.zeros((radial, width), F32)
    for k in range(parts):
        for c in part_of(k):
            c.wait()
        best = lax.fori_loop(k * CHUNK, (k + 1) * CHUNK, step, best)
    largest = jnp.max(best, axis=0, keepdims=True)
    largest = jnp.max(largest, axis=1, keepdims=True)
    for v in range(6):
        low, high = prim[v, 0], prim[v, count - 1]
        core[v] = jnp.where(even, high, low)
        up_send[v, :, :width] = jnp.where(even, low, high)
    top[...] = jnp.broadcast_to(largest.reshape(1, 1, 1), top.shape)


def shift_kernel(shift, came, sent, layer, out):
    radial, width = layer.shape[1], layer.shape[2]
    row = lax.axis_index("row")
    amount = shift[0] % width
    amount = jnp.where(row == 1, amount, jnp.where(row == 2, width - amount, 0))
    tiles = amount // LANES
    rest = amount % LANES
    lane = lax.broadcasted_iota(jnp.int32, (radial, LANES), 1)
    for v in range(6):
        parts = [
            pltpu.roll(ref[v, :, h * LANES : (h + 1) * LANES], rest, 1)
            for ref in (came, sent)
            for h in range(2)
        ]
        for t in range(2):
            picks = [
                jnp.where(lane < rest, parts[max(1 + t - q, 0)], parts[2 + t - q]) for q in range(3)
            ]
            out[v, :radial, t * LANES : (t + 1) * LANES] = jnp.where(
                tiles == 0, picks[0], jnp.where(tiles == 1, picks[1], picks[2])
            )
        out[v, radial:, :] = layer[v]


def weight_kernel(fwd, back, own, other, out):
    radial = out.shape[1]
    low = lax.axis_index("rad") == 0
    table = jnp.where(lax.axis_index("row") == 1, fwd[...], back[...])
    for v in range(6):
        mine, theirs = own[v, :radial], other[v, :radial]
        plane = jnp.concatenate([jnp.where(low, mine, theirs), jnp.where(low, theirs, mine)], 0)
        out[v] = jnp.dot(
            table, plane, precision=lax.Precision.HIGHEST, preferred_element_type=F32
        )


def closure(rho, nut, dist, grad2):
    strain = jnp.maximum(jnp.sqrt(0.25 * grad2), GRAD_FLOOR)
    ratio = (nut + NU_LAM) / (KAPPA * KAPPA * dist * dist * strain)
    eight = 8.0 * ratio
    shielding = 1.0 - jnp.tanh(eight * eight * eight)
    length = dist - shielding * jnp.maximum(0.0, dist - C_DES)
    quot = nut / length
    return shielding, rho * (CB1 * strain * nut - CW1 * (quot * quot))


def state_at(prim, der, a):
    return dict(
        rho=prim[0, a],
        u=[prim[1 + i, a] for i in range(3)],
        p=prim[4, a],
        m=[der[i, a] for i in range(3)],
        e=der[3, a],
        n=der[4, a],
        c=der[5, a],
    )


def face_kernel(
    rho_in, vel_in, press_in, nut_in, wall_in, core, layer, own_layer, wall_layer, came, col_next,
    col_own, top, flow_out, shield_out, edge_out,
    prim, der, wall, flow, shield,
    low_face, lay_hi, lay_lo, lay_u, azi_hi, azi_lo, azi_u, sems, out_sems,
):
    _, count, radial, width = prim.shape
    row, rad = lax.axis_index("row"), lax.axis_index("rad")
    even = row % 2 == 0
    at_low = rad == 0
    parts = count // CHUNK

    def part_of(k):
        rows = pl.ds(k * CHUNK, CHUNK)
        part = fetch((rho_in, vel_in, press_in, nut_in), prim, rows, sems.at[k])
        return part + [pltpu.make_async_copy(wall_in.at[rows], wall.at[rows], sems.at[k, 4])]

    def results_of(k):
        rows = pl.ds(k * CHUNK, CHUNK)
        return [
            pltpu.make_async_copy(flow.at[:, rows], flow_out.at[:, rows], out_sems.at[k, 0]),
            pltpu.make_async_copy(shield.at[rows], shield_out.at[rows], out_sems.at[k, 1]),
        ]

    for k in range(parts):
        for c in part_of(k):
            c.start()
    step_size = CFL / jnp.max(top[...])
    half = 0.5 * step_size
    sub = lax.broadcasted_iota(jnp.int32, (8, width), 0)
    lane = lax.broadcasted_iota(jnp.int32, (radial, LANES), 1)

    def derive(a):
        q = [prim[v, a] for v in range(6)]
        s = state_of(q)
        for i in range(3):
            der[i, a] = s["m"][i]
        der[3, a] = s["e"]
        der[4, a] = s["n"]
        der[5, a] = s["c"]

    def up_r(v, halo):
        lo, hi = pltpu.roll(v[:8], 7, 0), pltpu.roll(v[8:], 7, 0)
        edge = sub == 7
        return jnp.concatenate([jnp.where(edge, hi, lo), jnp.where(edge, halo, hi)], 0)

    def down_r(v, halo):
        lo, hi = pltpu.roll(v[:8], 1, 0), pltpu.roll(v[8:], 1, 0)
        edge = sub == 0
        return jnp.concatenate([jnp.where(edge, halo, lo), jnp.where(edge, lo, hi)], 0)

    def up_t(v, halo):
        lo, hi = pltpu.roll(v[:, :LANES], LANES - 1, 1), pltpu.roll(v[:, LANES:], LANES - 1, 1)
        edge = lane == LANES - 1
        return jnp.concatenate([jnp.where(edge, hi, lo), jnp.where(edge, halo, hi)], 1)

    def down_t(v, halo):
        lo, hi = pltpu.roll(v[:, :LANES], 1, 1), pltpu.roll(v[:, LANES:], 1, 1)
        edge = lane == 0
        return jnp.concatenate([jnp.where(edge, halo, lo), jnp.where(edge, lo, hi)], 1)

    def mirrored(q):
        return [q[0], q[1], -q[2], q[3], q[4], q[5]]

    got = [layer[v, radial:] for v in range(6)]
    bottom = [jnp.where(at_low, wall_layer[v], own_layer[v]) for v in range(6)]
    ceiling = [jnp.where(at_low, own_layer[v], wall_layer[v]) for v in range(6)]
    high = [jnp.where(at_low, g, w) for g, w in zip(got, mirrored(ceiling))]
    low = [jnp.where(at_low, w, g) for g, w in zip(got, mirrored(bottom))]
    high_state = pack_state(state_of(high))
    for i, name in enumerate(PASSED):
        lay_hi[i] = high_state[name]
    for i, f in enumerate(face_of(state_of(low), state_of(bottom), 1)):
        lay_lo[i] = f
    for i in range(3):
        lay_u[i] = low[1 + i]

    def column(ref, v):
        q = ref[v, :, ref.shape[2] - LANES :]
        return jnp.where(lane < count, q, 1.0)

    nxt_state = pack_state(state_of([column(col_next, v) for v in range(6)]))
    for i, name in enumerate(PASSED):
        azi_hi[i] = nxt_state[name]
    prev = [column(came, v) for v in range(6)]
    for i, f in enumerate(face_of(state_of(prev), state_of([column(col_own, v) for v in range(6)]), 2)):
        azi_lo[i] = f
    for i in range(3):
        azi_u[i] = prev[1 + i]

    end = [core[v] for v in range(6)]
    end_state = state_of(end)
    no_low = jnp.where(even, 0.0, 1.0)
    no_high = jnp.where(even, 1.0, 0.0)
    for c in part_of(0):
        c.wait()
    derive(0)
    for i, f in enumerate(face_of(end_state, state_at(prim, der, 0), 0)):
        low_face[i] = f * no_low

    def step(a, _):
        here = state_at(prim, der, a)
        last = a == count - 1
        first = a == 0
        later = jnp.minimum(a + 1, count - 1)
        earlier = jnp.maximum(a - 1, 0)
        total = [None] * 6
        derive(later)
        above = state_at(prim, der, later)
        right = dict(
            (k, [jnp.where(last, g, h) for g, h in zip(end_state[k], above[k])])
            if isinstance(above[k], list)
            else (k, jnp.where(last, end_state[k], above[k]))
            for k in above
        )
        keep = jnp.where(last, no_high, 1.0)
        for i, f in enumerate(face_of(here, right, 0)):
            f = f * keep
            total[i] = f - low_face[i]
            low_face[i] = f
        grad2 = None
        for i in range(3):
            down = jnp.where(first, end[1 + i], prim[1 + i, earlier])
            d = right["u"][i] - down
            grad2 = d * d if grad2 is None else grad2 + d * d
        outermost = jnp.where(even, first, last)
        grad2 = grad2 * jnp.where(outermost, 0.0, 1.0)
        packed = pack_state(here)
        row_of = pl.ds(a, 1)
        shifted = {n: up_r(packed[n], lay_hi[i, row_of, :]) for i, n in enumerate(PASSED)}
        face = face_of(here, unpack_state(shifted), 1)
        for i, f in enumerate(face):
            total[i] = total[i] + (f - down_r(f, lay_lo[i, row_of, :]))
        for i in range(3):
            d = shifted["u%d" % i] - down_r(here["u"][i], lay_u[i, row_of, :])
            grad2 = grad2 + d * d
        to_end = (LANES - 1) - a
        to_start = (LANES - a) % LANES
        shifted = {n: up_t(packed[n], pltpu.roll(azi_hi[i], to_end, 1)) for i, n in enumerate(PASSED)}
        face = face_of(here, unpack_state(shifted), 2)
        for i, f in enumerate(face):
            total[i] = total[i] + (f - down_t(f, pltpu.roll(azi_lo[i], to_start, 1)))
        for i in range(3):
            d = shifted["u%d" % i] - down_t(here["u"][i], pltpu.roll(azi_u[i], to_start, 1))
            grad2 = grad2 + d * d
        shielding, source = closure(here["rho"], prim[5, a], wall[a], grad2)
        cons = cons_of(here)
        for i in range(5):
            flow[i, a] = cons[i] - half * total[i]
        flow[5, a] = cons[5] - half * total[5] + step_size * source
        shield[a] = shielding

        @pl.when(outermost)
        def _():
            for i in range(6):
                edge_out[i] = cons[i] - half * total[i]
            edge_out[6] = grad2
            edge_out[7] = wall[a]
            inside = jnp.where(even, 1, count - 2)
            for i in range(3):
                edge_out[8 + i] = prim[1 + i, inside]
            edge_out[11] = jnp.zeros((radial, width), F32) + step_size

        return 0

    def part_step(k, _):
        @pl.when(k + 1 < parts)
        def _():
            for c in part_of(k + 1):
                c.wait()

        lax.fori_loop(k * CHUNK, (k + 1) * CHUNK, step, 0)
        for c in results_of(k):
            c.start()
        return 0

    lax.fori_loop(0, parts, part_step, 0)
    for k in range(parts):
        for c in results_of(k):
            c.wait()


def edge_kernel(
    flow_in, shield_in, edge, sent, ghost, flow_out, shield_out, edge_flow, edge_shield, sems
):
    del flow_in, shield_in
    _, radial, width = ghost.shape
    count = shield_out.shape[0]
    row = lax.axis_index("row")
    even = row % 2 == 0
    coupled = (row == 1) | (row == 2)
    step_size = edge[11]
    end = jnp.where(even, 0, count - 1)
    mine = [sent[v, :, :width] for v in range(6)]
    beyond = [jnp.where(coupled, ghost[v], mine[v]) for v in range(6)]
    here, out_state = state_of(mine), state_of(beyond)
    grad2 = edge[6]
    for i in range(3):
        d = edge[8 + i] - beyond[1 + i]
        grad2 = grad2 + d * d

    def pick(p, q):
        return dict(
            (k, [jnp.where(even, x, y) for x, y in zip(p[k], q[k])])
            if isinstance(p[k], list)
            else (k, jnp.where(even, p[k], q[k]))
            for k in p
        )

    shielding, source = closure(here["rho"], mine[5], edge[7], grad2)
    edge_shield[...] = shielding
    sign = jnp.where(even, -0.5, 0.5)
    for i, f in enumerate(face_of(pick(out_state, here), pick(here, out_state), 0)):
        value = edge[i] - step_size * (sign * f)
        edge_flow[i] = value + step_size * source if i == 5 else value
    copies = [
        pltpu.make_async_copy(edge_flow, flow_out.at[:, end], sems.at[0]),
        pltpu.make_async_copy(edge_shield, shield_out.at[end], sems.at[1]),
    ]
    for c in copies:
        c.start()
    for c in copies:
        c.wait()


def body(density, velocity, pressure, nu_tilde, wall_distance, interp_fwd, interp_back, offset):
    rows, rads, cycle = (lax.axis_size(n) for n in AXES)
    count, radial, width = density.shape

    def device(row, rad, azi):
        return (row * rads + rad) * cycle + azi % cycle

    def everyone(target):
        return [
            (device(r, d, a), target(r, d, a))
            for r in range(rows)
            for d in range(rads)
            for a in range(cycle)
        ]

    plane = shaped(6, radial, width)
    wide = shaped(6, radial, width + LANES)
    column = shaped(6, radial, LANES)
    devices = rows * rads * cycle
    whole = (6, count, radial, width)
    parts = count // CHUNK
    fields = [far_away(x) for x in (density, velocity, pressure, nu_tilde)]
    dma = pltpu.SemaphoreType.DMA
    core, up_send, layer, far_layer, col_down, top = pl.pallas_call(
        derive_kernel,
        out_shape=(
            plane, wide, shaped(6, count, width), shaped(6, count, width), column,
            shaped(devices, 1, LANES),
        ),
        in_specs=[HBM] * 4,
        out_specs=(VMEM,) * 6,
        scratch_shapes=[pltpu.VMEM(whole, F32), dma((parts, 4))],
        compiler_params=params(),
        name="derive",
    )(*fields)

    up = everyone(lambda r, d, a: device(r, d, a + 1))
    down = everyone(lambda r, d, a: device(r, d, a - 1))
    pair = everyone(lambda r, d, a: device(r ^ 1, d, a))
    across = everyone(lambda r, d, a: device(r, rads - 1 - d, a))
    tops = lax.all_to_all(top, AXES, 0, 0)
    came = lax.ppermute(up_send, AXES, up)
    col_next = lax.ppermute(col_down, AXES, down)
    core_got = lax.ppermute(core, AXES, pair)

    moved = pl.pallas_call(
        shift_kernel,
        out_shape=shaped(6, radial + count, width),
        in_specs=[SMEM, VMEM, VMEM, VMEM],
        out_specs=VMEM,
        compiler_params=params(),
        name="shift",
    )(offset, came, up_send, layer)
    swapped = lax.ppermute(moved, AXES, across)
    weighted = pl.pallas_call(
        weight_kernel,
        out_shape=plane,
        in_specs=[VMEM] * 4,
        out_specs=VMEM,
        compiler_params=params(),
        name="weigh",
    )(interp_fwd, interp_back, moved, swapped)

    faces = pl.pallas_call(
        face_kernel,
        out_shape=(apart(*whole), apart(count, radial, width), shaped(12, radial, width)),
        in_specs=[HBM] * 5 + [VMEM] * 8,
        out_specs=(HBM, HBM, VMEM),
        scratch_shapes=[
            pltpu.VMEM(whole, F32),
            pltpu.VMEM(whole, F32),
            pltpu.VMEM((count, radial, width), F32),
            pltpu.VMEM(whole, F32),
            pltpu.VMEM((count, radial, width), F32),
            pltpu.VMEM((6, radial, width), F32),
            pltpu.VMEM((8, count, width), F32),
            pltpu.VMEM((6, count, width), F32),
            pltpu.VMEM((3, count, width), F32),
            pltpu.VMEM((8, radial, LANES), F32),
            pltpu.VMEM((6, radial, LANES), F32),
            pltpu.VMEM((3, radial, LANES), F32),
            dma((parts, 5)),
            dma((parts, 2)),
        ],
        compiler_params=params(),
        cost_estimate=pl.CostEstimate(
            flops=25_000_000, bytes_accessed=6_000_000, transcendentals=300_000
        ),
        name="faces",
    )

    def far(blocks):
        route = []
        for d in range(rads):
            for a in range(cycle):
                route.append((device(1, d, a), device(2, d, a + blocks)))
                route.append((device(2, d, a), device(1, d, a + cycle - 1 - blocks)))

        def branch(block, arrays, *rest):
            return lax.ppermute(block, AXES, route), faces(*map(far_away, arrays), *rest)

        return branch

    ghost, (flow, shield, edge) = lax.switch(
        offset[0] // width,
        [far(b) for b in range(cycle)],
        weighted, (density, velocity, pressure, nu_tilde, wall_distance),
        core_got, swapped, layer, far_layer, came, col_next, col_down, tops,
    )

    return pl.pallas_call(
        edge_kernel,
        out_shape=(shaped(*whole), shaped(count, radial, width)),
        in_specs=[HBM] * 2 + [VMEM] * 3,
        out_specs=(HBM, HBM),
        input_output_aliases={0: 0, 1: 1},
        scratch_shapes=[
            pltpu.VMEM((6, radial, width), F32),
            pltpu.VMEM((radial, width), F32),
            dma((2,)),
        ],
        compiler_params=params(),
        name="edge",
    )(far_away(flow), far_away(shield), edge, up_send, ghost)


def solution(mesh):
    placed = (
        P("row", "rad", "azi"),
        P(None, "row", "rad", "azi"),
        P("row", "rad", "azi"),
        P("row", "rad", "azi"),
        P("row", "rad", "azi"),
        P("rad", None),
        P("rad", None),
        P(),
    )
    return jax.shard_map(
        body,
        mesh=mesh,
        in_specs=placed,
        out_specs=(P(None, "row", "rad", "azi"), P("row", "rad", "azi")),
        check_vma=False,
    )
```

```python
import functools

import jax
import jax.numpy as jnp
from jax import lax
from jax.experimental import pallas as pl
from jax.experimental.pallas import tpu as pltpu
from jax.sharding import PartitionSpec as P

GAMMA = 1.4
CFL = 0.8
KAPPA = 0.41
C_DES = 0.65
CB1 = 0.1355
CW1 = 3.239
NU_LAM = 0.001
GRAD_FLOOR = 0.2

AXES = ("row", "rad", "azi")
LANES = 128
CHUNK = 4
F32 = jnp.float32
VMEM = pl.BlockSpec(memory_space=pltpu.VMEM)
SMEM = pl.BlockSpec(memory_space=pltpu.SMEM)
HBM = pl.BlockSpec(memory_space=pltpu.HBM)


def params(mib=32):
    return pltpu.CompilerParams(vmem_limit_bytes=mib * 1024 * 1024)


def shaped(*dims):
    return jax.ShapeDtypeStruct(dims, F32)


def apart(*dims):
    return pltpu.HBM(dims, F32)


def far_away(array):
    return pltpu.with_memory_space_constraint(array, pltpu.HBM)


def sound_speed(rho, press):
    scaled = GAMMA * press
    return scaled * lax.rsqrt(scaled * rho)


def energy_of(press, m, u):
    return press * (1.0 / (GAMMA - 1.0)) + 0.5 * (m[0] * u[0] + m[1] * u[1] + m[2] * u[2])


def state_of(prim):
    rho, u, press, nut = prim[0], prim[1:4], prim[4], prim[5]
    m = [rho * v for v in u]
    return dict(
        rho=rho, m=m, u=u, p=press, e=energy_of(press, m, u), n=rho * nut, c=sound_speed(rho, press)
    )


def cons_of(s):
    return [s["rho"], s["m"][0], s["m"][1], s["m"][2], s["e"], s["n"]]


def flux_of(s, k):
    w = s["u"][k]
    mom = [s["m"][k] * s["u"][i] for i in range(3)]
    mom[k] = mom[k] + s["p"]
    return [s["m"][k], mom[0], mom[1], mom[2], (s["e"] + s["p"]) * w, s["n"] * w]


def face_of(left, right, k):
    wave = jnp.maximum(jnp.abs(left["u"][k]) + left["c"], jnp.abs(right["u"][k]) + right["c"])
    return [
        (fl + fr) - wave * (ur - ul)
        for fl, fr, ul, ur in zip(
            flux_of(left, k), flux_of(right, k), cons_of(left), cons_of(right)
        )
    ]


NAMES = ("rho", "u0", "u1", "u2", "p", "m0", "m1", "m2", "e", "n", "c")
PASSED = ("rho", "u0", "u1", "u2", "p", "e", "n", "c")


def pack_state(s):
    return dict(
        rho=s["rho"], u0=s["u"][0], u1=s["u"][1], u2=s["u"][2], p=s["p"], e=s["e"], n=s["n"], c=s["c"]
    )


def unpack_state(d):
    u = [d["u0"], d["u1"], d["u2"]]
    return dict(rho=d["rho"], u=u, m=[d["rho"] * v for v in u], p=d["p"], e=d["e"], n=d["n"], c=d["c"])


def fetch(sources, prim, rows, sems):
    rho, vel, press, nut = sources
    return [
        pltpu.make_async_copy(rho.at[rows], prim.at[0, rows], sems.at[0]),
        pltpu.make_async_copy(vel.at[:, rows], prim.at[pl.ds(1, 3), rows], sems.at[1]),
        pltpu.make_async_copy(press.at[rows], prim.at[4, rows], sems.at[2]),
        pltpu.make_async_copy(nut.at[rows], prim.at[5, rows], sems.at[3]),
    ]


def derive_kernel(
    rho_in, vel_in, press_in, nut_in, core, up_send, layer, far_layer, cols, top, prim, sems,
):
    _, count, radial, width = prim.shape
    even = lax.axis_index("row") % 2 == 0
    inner_rad = lax.axis_index("rad") == 0
    lane = lax.broadcasted_iota(jnp.int32, (radial, LANES), 1)
    parts = count // CHUNK

    def part_of(k):
        return fetch((rho_in, vel_in, press_in, nut_in), prim, pl.ds(k * CHUNK, CHUNK), sems.at[k])

    for k in range(parts):
        for c in part_of(k):
            c.start()
    cols[...] = jnp.zeros(cols.shape, F32)

    def step(a, best):
        speed = 3.0 * sound_speed(prim[0, a], prim[4, a])
        here = lane // 2 == a
        for v in range(6):
            plane = prim[v, a]
            if 1 <= v <= 3:
                speed = speed + jnp.abs(plane)
            high, low = plane[radial - 1 :], plane[:1]
            layer[v, pl.ds(a, 1), :] = jnp.where(inner_rad, high, low)
            far_layer[v, pl.ds(a, 1), :] = jnp.where(inner_rad, low, high)
            first, last = plane[:, :LANES], plane[:, width - LANES :]
            both = pltpu.roll(jnp.where(lane == 0, first, last), 2 * a + 1, 1)
            cols[v] = jnp.where(here, both, cols[v])
        return jnp.maximum(best, speed)

    best = jnp.zeros((radial, width), F32)
    for k in range(parts):
        for c in part_of(k):
            c.wait()
        best = lax.fori_loop(k * CHUNK, (k + 1) * CHUNK, step, best)
    largest = jnp.max(best, axis=0, keepdims=True)
    largest = jnp.max(largest, axis=1, keepdims=True)
    for v in range(6):
        low, high = prim[v, 0], prim[v, count - 1]
        core[v] = jnp.where(even, high, low)
        up_send[v, :, :width] = jnp.where(even, low, high)
        up_send[v, :, width:] = cols[v]
    top[...] = jnp.broadcast_to(largest.reshape(1, 1, 1), top.shape)


def shift_kernel(shift, came, sent, layer, out):
    radial, width = layer.shape[1], layer.shape[2]
    row = lax.axis_index("row")
    amount = shift[0] % width
    amount = jnp.where(row == 1, amount, jnp.where(row == 2, width - amount, 0))
    tiles = amount // LANES
    rest = amount % LANES
    lane = lax.broadcasted_iota(jnp.int32, (radial, LANES), 1)
    for v in range(6):
        parts = [
            pltpu.roll(ref[v, :, h * LANES : (h + 1) * LANES], rest, 1)
            for ref in (came, sent)
            for h in range(2)
        ]
        for t in range(2):
            picks = [
                jnp.where(lane < rest, parts[max(1 + t - q, 0)], parts[2 + t - q]) for q in range(3)
            ]
            out[v, :radial, t * LANES : (t + 1) * LANES] = jnp.where(
                tiles == 0, picks[0], jnp.where(tiles == 1, picks[1], picks[2])
            )
        out[v, radial:, :] = layer[v]


def weight_kernel(fwd, back, own, other, out):
    radial = out.shape[1]
    low = lax.axis_index("rad") == 0
    table = jnp.where(lax.axis_index("row") == 1, fwd[...], back[...])
    for v in range(6):
        mine, theirs = own[v, :radial], other[v, :radial]
        plane = jnp.concatenate([jnp.where(low, mine, theirs), jnp.where(low, theirs, mine)], 0)
        out[v] = jnp.dot(
            table, plane, precision=lax.Precision.HIGHEST, preferred_element_type=F32
        )


def closure(rho, nut, dist, grad2):
    square = jnp.maximum(0.25 * grad2, GRAD_FLOOR * GRAD_FLOOR)
    inverse = lax.rsqrt(square)
    strain = square * inverse
    eight = (8.0 / (KAPPA * KAPPA)) * (nut + NU_LAM) * inverse / (dist * dist)
    shielding = 1.0 - jnp.tanh(eight * eight * eight)
    length = dist - shielding * jnp.maximum(0.0, dist - C_DES)
    quot = nut / length
    return shielding, rho * (CB1 * strain * nut - CW1 * (quot * quot))


def state_at(prim, der, a):
    return dict(
        rho=prim[0, a],
        u=[prim[1 + i, a] for i in range(3)],
        p=prim[4, a],
        m=[der[i, a] for i in range(3)],
        e=der[3, a],
        n=der[4, a],
        c=der[5, a],
    )


def face_kernel(
    prim, wall_in, core, layer, own_layer, wall_layer, came, col_next,
    col_own, top, flow_out, shield_out, edge_out,
    der, wall, flow, shield,
    low_face, lay_hi, lay_lo, lay_u, azi_hi, azi_lo, azi_u, sems, out_sems,
):
    _, count, radial, width = prim.shape
    row, rad = lax.axis_index("row"), lax.axis_index("rad")
    even = row % 2 == 0
    at_low = rad == 0
    parts = count // CHUNK

    def part_of(k):
        rows = pl.ds(k * CHUNK, CHUNK)
        return [pltpu.make_async_copy(wall_in.at[rows], wall.at[rows], sems.at[k])]

    def results_of(k):
        rows = pl.ds(k * CHUNK, CHUNK)
        return [
            pltpu.make_async_copy(flow.at[:, rows], flow_out.at[:, rows], out_sems.at[k, 0]),
            pltpu.make_async_copy(shield.at[rows], shield_out.at[rows], out_sems.at[k, 1]),
        ]

    for k in range(parts):
        for c in part_of(k):
            c.start()
    step_size = CFL / jnp.max(top[...])
    half = 0.5 * step_size
    sub = lax.broadcasted_iota(jnp.int32, (8, width), 0)
    lane = lax.broadcasted_iota(jnp.int32, (radial, LANES), 1)

    def derive(a):
        q = [prim[v, a] for v in range(6)]
        s = state_of(q)
        for i in range(3):
            der[i, a] = s["m"][i]
        der[3, a] = s["e"]
        der[4, a] = s["n"]
        der[5, a] = s["c"]

    def up_r(v, halo):
        lo, hi = pltpu.roll(v[:8], 7, 0), pltpu.roll(v[8:], 7, 0)
        edge = sub == 7
        return jnp.concatenate([jnp.where(edge, hi, lo), jnp.where(edge, halo, hi)], 0)

    def down_r(v, halo):
        lo, hi = pltpu.roll(v[:8], 1, 0), pltpu.roll(v[8:], 1, 0)
        edge = sub == 0
        return jnp.concatenate([jnp.where(edge, halo, lo), jnp.where(edge, lo, hi)], 0)

    def up_t(v, halo):
        lo, hi = pltpu.roll(v[:, :LANES], LANES - 1, 1), pltpu.roll(v[:, LANES:], LANES - 1, 1)
        edge = lane == LANES - 1
        return jnp.concatenate([jnp.where(edge, hi, lo), jnp.where(edge, halo, hi)], 1)

    def down_t(v, halo):
        lo, hi = pltpu.roll(v[:, :LANES], 1, 1), pltpu.roll(v[:, LANES:], 1, 1)
        edge = lane == 0
        return jnp.concatenate([jnp.where(edge, halo, lo), jnp.where(edge, lo, hi)], 1)

    def mirrored(q):
        return [q[0], q[1], -q[2], q[3], q[4], q[5]]

    got = [layer[v, radial:] for v in range(6)]
    bottom = [jnp.where(at_low, wall_layer[v], own_layer[v]) for v in range(6)]
    ceiling = [jnp.where(at_low, own_layer[v], wall_layer[v]) for v in range(6)]
    high = [jnp.where(at_low, g, w) for g, w in zip(got, mirrored(ceiling))]
    low = [jnp.where(at_low, w, g) for g, w in zip(got, mirrored(bottom))]
    high_state = pack_state(state_of(high))
    for i, name in enumerate(PASSED):
        lay_hi[i] = high_state[name]
    for i, f in enumerate(face_of(state_of(low), state_of(bottom), 1)):
        lay_lo[i] = f
    for i in range(3):
        lay_u[i] = low[1 + i]

    def column(ref, v):
        q = ref[v, :, ref.shape[2] - LANES :]
        return jnp.where(lane < 2 * count, q, 1.0)

    nxt_state = pack_state(state_of([column(col_next, v) for v in range(6)]))
    for i, name in enumerate(PASSED):
        azi_hi[i] = nxt_state[name]
    prev = [column(came, v) for v in range(6)]
    for i, f in enumerate(face_of(state_of(prev), state_of([pltpu.roll(column(col_own, v), LANES - 1, 1) for v in range(6)]), 2)):
        azi_lo[i] = f
    for i in range(3):
        azi_u[i] = prev[1 + i]

    end = [core[v] for v in range(6)]
    end_state = state_of(end)
    no_low = jnp.where(even, 0.0, 1.0)
    no_high = jnp.where(even, 1.0, 0.0)
    for c in part_of(0):
        c.wait()
    derive(0)
    for i, f in enumerate(face_of(end_state, state_at(prim, der, 0), 0)):
        low_face[i] = f * no_low

    def step(a, _):
        here = state_at(prim, der, a)
        last = a == count - 1
        first = a == 0
        later = jnp.minimum(a + 1, count - 1)
        earlier = jnp.maximum(a - 1, 0)
        total = [None] * 6
        derive(later)
        above = state_at(prim, der, later)
        right = dict(
            (k, [jnp.where(last, g, h) for g, h in zip(end_state[k], above[k])])
            if isinstance(above[k], list)
            else (k, jnp.where(last, end_state[k], above[k]))
            for k in above
        )
        keep = jnp.where(last, no_high, 1.0)
        for i, f in enumerate(face_of(here, right, 0)):
            f = f * keep
            total[i] = f - low_face[i]
            low_face[i] = f
        grad2 = None
        for i in range(3):
            down = jnp.where(first, end[1 + i], prim[1 + i, earlier])
            d = right["u"][i] - down
            grad2 = d * d if grad2 is None else grad2 + d * d
        outermost = jnp.where(even, first, last)
        grad2 = grad2 * jnp.where(outermost, 0.0, 1.0)
        packed = pack_state(here)
        row_of = pl.ds(a, 1)
        shifted = {n: up_r(packed[n], lay_hi[i, row_of, :]) for i, n in enumerate(PASSED)}
        face = face_of(here, unpack_state(shifted), 1)
        for i, f in enumerate(face):
            total[i] = total[i] + (f - down_r(f, lay_lo[i, row_of, :]))
        for i in range(3):
            d = shifted["u%d" % i] - down_r(here["u"][i], lay_u[i, row_of, :])
            grad2 = grad2 + d * d
        to_end = (LANES - 2) - 2 * a
        to_start = (LANES - 2 * a) % LANES
        shifted = {n: up_t(packed[n], pltpu.roll(azi_hi[i], to_end, 1)) for i, n in enumerate(PASSED)}
        face = face_of(here, unpack_state(shifted), 2)
        for i, f in enumerate(face):
            total[i] = total[i] + (f - down_t(f, pltpu.roll(azi_lo[i], to_start, 1)))
        for i in range(3):
            d = shifted["u%d" % i] - down_t(here["u"][i], pltpu.roll(azi_u[i], to_start, 1))
            grad2 = grad2 + d * d
        shielding, source = closure(here["rho"], prim[5, a], wall[a], grad2)
        cons = cons_of(here)
        for i in range(5):
            flow[i, a] = cons[i] - half * total[i]
        flow[5, a] = cons[5] - half * total[5] + step_size * source
        shield[a] = shielding

        @pl.when(outermost)
        def _():
            for i in range(6):
                edge_out[i] = cons[i] - half * total[i]
            edge_out[6] = grad2
            edge_out[7] = wall[a]
            inside = jnp.where(even, 1, count - 2)
            for i in range(3):
                edge_out[8 + i] = prim[1 + i, inside]
            edge_out[11] = jnp.zeros((radial, width), F32) + step_size

        return 0

    def part_step(k, _):
        @pl.when(k + 1 < parts)
        def _():
            for c in part_of(k + 1):
                c.wait()

        lax.fori_loop(k * CHUNK, (k + 1) * CHUNK, step, 0)
        for c in results_of(k):
            c.start()
        return 0

    lax.fori_loop(0, parts, part_step, 0)
    for k in range(parts):
        for c in results_of(k):
            c.wait()


def edge_kernel(
    flow_in, shield_in, edge, sent, ghost, flow_out, shield_out, edge_flow, edge_shield, sems
):
    del flow_in, shield_in
    _, radial, width = ghost.shape
    count = shield_out.shape[0]
    row = lax.axis_index("row")
    even = row % 2 == 0
    coupled = (row == 1) | (row == 2)
    end = jnp.where(even, 0, count - 1)
    step_size = edge[11]
    mine = [sent[v, :, :width] for v in range(6)]
    beyond = [jnp.where(coupled, ghost[v], mine[v]) for v in range(6)]
    here, out_state = state_of(mine), state_of(beyond)
    grad2 = edge[6]
    for i in range(3):
        d = edge[8 + i] - beyond[1 + i]
        grad2 = grad2 + d * d

    def pick(p, q):
        return dict(
            (k, [jnp.where(even, x, y) for x, y in zip(p[k], q[k])])
            if isinstance(p[k], list)
            else (k, jnp.where(even, p[k], q[k]))
            for k in p
        )

    shielding, source = closure(here["rho"], mine[5], edge[7], grad2)
    edge_shield[...] = shielding
    sign = jnp.where(even, -0.5, 0.5)
    for i, f in enumerate(face_of(pick(out_state, here), pick(here, out_state), 0)):
        value = edge[i] - step_size * (sign * f)
        edge_flow[i] = value + step_size * source if i == 5 else value
    copies = [
        pltpu.make_async_copy(edge_flow, flow_out.at[:, end], sems.at[0]),
        pltpu.make_async_copy(edge_shield, shield_out.at[end], sems.at[1]),
    ]
    for c in copies:
        c.start()
    for c in copies:
        c.wait()


def derive_call(fields, devices):
    count, radial, width = fields[0].shape
    plane, layer = shaped(6, radial, width), shaped(6, count, width)
    return pl.pallas_call(
        derive_kernel,
        out_shape=(
            plane, shaped(6, radial, width + LANES), layer, layer, shaped(6, radial, LANES),
            shaped(devices, 1, LANES), pltpu.VMEM((6, count, radial, width), F32),
        ),
        in_specs=[HBM] * 4,
        out_specs=(VMEM,) * 7,
        scratch_shapes=[pltpu.SemaphoreType.DMA((count // CHUNK, 4))],
        compiler_params=params(),
        name="derive",
    )(*fields)


def faces_call(*arrays):
    whole = arrays[0].shape
    _, count, radial, width = whole
    parts = count // CHUNK
    return pl.pallas_call(
        face_kernel,
        out_shape=(apart(*whole), apart(count, radial, width), shaped(12, radial, width)),
        in_specs=[VMEM, HBM] + [VMEM] * 8,
        out_specs=(HBM, HBM, VMEM),
        scratch_shapes=[
            pltpu.VMEM(whole, F32),
            pltpu.VMEM((count, radial, width), F32),
            pltpu.VMEM(whole, F32),
            pltpu.VMEM((count, radial, width), F32),
            pltpu.VMEM((6, radial, width), F32),
            pltpu.VMEM((8, count, width), F32),
            pltpu.VMEM((6, count, width), F32),
            pltpu.VMEM((3, count, width), F32),
            pltpu.VMEM((8, radial, LANES), F32),
            pltpu.VMEM((6, radial, LANES), F32),
            pltpu.VMEM((3, radial, LANES), F32),
            pltpu.SemaphoreType.DMA((parts,)),
            pltpu.SemaphoreType.DMA((parts, 2)),
        ],
        compiler_params=params(),
        cost_estimate=pl.CostEstimate(
            flops=25_000_000, bytes_accessed=6_000_000, transcendentals=300_000
        ),
        name="faces",
    )(*arrays)


def edge_call(flow, shield, edge, sent, ghost):
    _, radial, width = ghost.shape
    return pl.pallas_call(
        edge_kernel,
        out_shape=(shaped(*flow.shape), shaped(*shield.shape)),
        in_specs=[HBM] * 2 + [VMEM] * 3,
        out_specs=(HBM, HBM),
        input_output_aliases={0: 0, 1: 1},
        scratch_shapes=[
            pltpu.VMEM((6, radial, width), F32),
            pltpu.VMEM((radial, width), F32),
            pltpu.SemaphoreType.DMA((2,)),
        ],
        compiler_params=params(),
        name="edge",
    )(flow, shield, edge, sent, ghost)


def body(density, velocity, pressure, nu_tilde, wall_distance, interp_fwd, interp_back, offset):
    rows, rads, cycle = (lax.axis_size(n) for n in AXES)
    count, radial, width = density.shape

    def device(row, rad, azi):
        return (row * rads + rad) * cycle + azi % cycle

    def everyone(target):
        return [
            (device(r, d, a), target(r, d, a))
            for r in range(rows)
            for d in range(rads)
            for a in range(cycle)
        ]

    plane = shaped(6, radial, width)
    devices = rows * rads * cycle
    fields = [far_away(x) for x in (density, velocity, pressure, nu_tilde)]
    core, up_send, layer, far_layer, cols, top, prim = derive_call(fields, devices)

    up = everyone(lambda r, d, a: device(r, d, a + 1))
    down = everyone(lambda r, d, a: device(r, d, a - 1))
    pair = everyone(lambda r, d, a: device(r ^ 1, d, a))
    across = everyone(lambda r, d, a: device(r, rads - 1 - d, a))
    tops = lax.all_to_all(top, AXES, 0, 0)
    came = lax.ppermute(up_send, AXES, up)
    col_next = lax.ppermute(cols, AXES, down)
    core_got = lax.ppermute(core, AXES, pair)

    moved = pl.pallas_call(
        shift_kernel,
        out_shape=shaped(6, radial + count, width),
        in_specs=[SMEM, VMEM, VMEM, VMEM],
        out_specs=VMEM,
        compiler_params=params(),
        name="shift",
    )(offset, came, up_send, layer)
    swapped = lax.ppermute(moved, AXES, across)
    weighted = pl.pallas_call(
        weight_kernel,
        out_shape=plane,
        in_specs=[VMEM] * 4,
        out_specs=VMEM,
        compiler_params=params(),
        name="weigh",
    )(interp_fwd, interp_back, moved, swapped)

    def far(blocks):
        route = []
        for d in range(rads):
            for a in range(cycle):
                route.append((device(1, d, a), device(2, d, a + blocks)))
                route.append((device(2, d, a), device(1, d, a + cycle - 1 - blocks)))

        def branch(block, sent, near, dist, *rest):
            near = pltpu.with_memory_space_constraint(near, pltpu.VMEM)
            ghost = lax.ppermute(block, AXES, route)
            flow, shield, edge = faces_call(near, far_away(dist), *rest)
            return edge_call(far_away(flow), far_away(shield), edge, sent, ghost)

        return branch

    return lax.switch(
        offset[0] // width,
        [far(b) for b in range(cycle)],
        weighted, up_send, prim, wall_distance,
        core_got, swapped, layer, far_layer, came, col_next, cols, tops,
    )


def solution(mesh):
    placed = (
        P("row", "rad", "azi"),
        P(None, "row", "rad", "azi"),
        P("row", "rad", "azi"),
        P("row", "rad", "azi"),
        P("row", "rad", "azi"),
        P("rad", None),
        P("rad", None),
        P(),
    )
    return jax.shard_map(
        body,
        mesh=mesh,
        in_specs=placed,
        out_specs=(P(None, "row", "rad", "azi"), P("row", "rad", "azi")),
        check_vma=False,
    )
```

```python
import functools

import jax
import jax.numpy as jnp
from jax import lax
from jax.experimental import pallas as pl
from jax.experimental.pallas import tpu as pltpu
from jax.sharding import PartitionSpec as P

GAMMA = 1.4
CFL = 0.8
KAPPA = 0.41
C_DES = 0.65
CB1 = 0.1355
CW1 = 3.239
NU_LAM = 0.001
GRAD_FLOOR = 0.2

AXES = ("row", "rad", "azi")
LANES = 128
CHUNK = 4
F32 = jnp.float32
VMEM = pl.BlockSpec(memory_space=pltpu.VMEM)
SMEM = pl.BlockSpec(memory_space=pltpu.SMEM)
HBM = pl.BlockSpec(memory_space=pltpu.HBM)


def params(mib=32):
    return pltpu.CompilerParams(vmem_limit_bytes=mib * 1024 * 1024)


def shaped(*dims):
    return jax.ShapeDtypeStruct(dims, F32)


def apart(*dims):
    return pltpu.HBM(dims, F32)


def far_away(array):
    return pltpu.with_memory_space_constraint(array, pltpu.HBM)


def sound_speed(rho, press):
    scaled = GAMMA * press
    return scaled * lax.rsqrt(scaled * rho)


def energy_of(press, m, u):
    return press * (1.0 / (GAMMA - 1.0)) + 0.5 * (m[0] * u[0] + m[1] * u[1] + m[2] * u[2])


def state_of(prim):
    rho, u, press, nut = prim[0], prim[1:4], prim[4], prim[5]
    m = [rho * v for v in u]
    return dict(
        rho=rho, m=m, u=u, p=press, e=energy_of(press, m, u), n=rho * nut, c=sound_speed(rho, press)
    )


def ghost_state_of(prim):
    rho, u, press, nut = prim[0], prim[1:4], prim[4], prim[5]
    kinetic = 0.5 * rho * (u[0] * u[0] + u[1] * u[1] + u[2] * u[2])
    return dict(
        rho=rho, m=[rho * v for v in u], u=u, p=press, e=press / (GAMMA - 1.0) + kinetic, n=rho * nut,
        c=jnp.sqrt(GAMMA * press / rho),
    )


def cons_of(s):
    return [s["rho"], s["m"][0], s["m"][1], s["m"][2], s["e"], s["n"]]


def flux_of(s, k):
    w = s["u"][k]
    mom = [s["m"][k] * s["u"][i] for i in range(3)]
    mom[k] = mom[k] + s["p"]
    return [s["m"][k], mom[0], mom[1], mom[2], (s["e"] + s["p"]) * w, s["n"] * w]


def face_of(left, right, k):
    wave = jnp.maximum(jnp.abs(left["u"][k]) + left["c"], jnp.abs(right["u"][k]) + right["c"])
    return [
        (fl + fr) - wave * (ur - ul)
        for fl, fr, ul, ur in zip(
            flux_of(left, k), flux_of(right, k), cons_of(left), cons_of(right)
        )
    ]


def ghost_face_of(left, right, k):
    wave = jnp.maximum(jnp.abs(left["u"][k]) + left["c"], jnp.abs(right["u"][k]) + right["c"])
    return [
        0.5 * (fl + fr) - 0.5 * wave * (ur - ul)
        for fl, fr, ul, ur in zip(
            flux_of(left, k), flux_of(right, k), cons_of(left), cons_of(right)
        )
    ]


NAMES = ("rho", "u0", "u1", "u2", "p", "m0", "m1", "m2", "e", "n", "c")
PASSED = ("rho", "u0", "u1", "u2", "p", "e", "n", "c")


def pack_state(s):
    return dict(
        rho=s["rho"], u0=s["u"][0], u1=s["u"][1], u2=s["u"][2], p=s["p"], e=s["e"], n=s["n"], c=s["c"]
    )


def unpack_state(d):
    u = [d["u0"], d["u1"], d["u2"]]
    return dict(rho=d["rho"], u=u, m=[d["rho"] * v for v in u], p=d["p"], e=d["e"], n=d["n"], c=d["c"])


def fetch(sources, prim, rows, sems):
    rho, vel, press, nut = sources
    return [
        pltpu.make_async_copy(rho.at[rows], prim.at[0, rows], sems.at[0]),
        pltpu.make_async_copy(vel.at[:, rows], prim.at[pl.ds(1, 3), rows], sems.at[1]),
        pltpu.make_async_copy(press.at[rows], prim.at[4, rows], sems.at[2]),
        pltpu.make_async_copy(nut.at[rows], prim.at[5, rows], sems.at[3]),
    ]


def derive_kernel(
    rho_in, vel_in, press_in, nut_in, core, up_send, layer, far_layer, cols, top, prim, sems,
):
    _, count, radial, width = prim.shape
    even = lax.axis_index("row") % 2 == 0
    inner_rad = lax.axis_index("rad") == 0
    lane = lax.broadcasted_iota(jnp.int32, (radial, LANES), 1)
    parts = count // CHUNK

    def part_of(k):
        return fetch((rho_in, vel_in, press_in, nut_in), prim, pl.ds(k * CHUNK, CHUNK), sems.at[k])

    for k in range(parts):
        for c in part_of(k):
            c.start()
    cols[...] = jnp.zeros(cols.shape, F32)

    def step(a, best):
        speed = 3.0 * sound_speed(prim[0, a], prim[4, a])
        here = lane // 2 == a
        for v in range(6):
            plane = prim[v, a]
            if 1 <= v <= 3:
                speed = speed + jnp.abs(plane)
            high, low = plane[radial - 1 :], plane[:1]
            layer[v, pl.ds(a, 1), :] = jnp.where(inner_rad, high, low)
            far_layer[v, pl.ds(a, 1), :] = jnp.where(inner_rad, low, high)
            first, last = plane[:, :LANES], plane[:, width - LANES :]
            both = pltpu.roll(jnp.where(lane == 0, first, last), 2 * a + 1, 1)
            cols[v] = jnp.where(here, both, cols[v])
        return jnp.maximum(best, speed)

    best = jnp.zeros((radial, width), F32)
    for k in range(parts):
        for c in part_of(k):
            c.wait()
        for j in range(CHUNK):
            best = step(k * CHUNK + j, best)
    largest = jnp.max(best, axis=0, keepdims=True)
    largest = jnp.max(largest, axis=1, keepdims=True)
    for v in range(6):
        low, high = prim[v, 0], prim[v, count - 1]
        core[v] = jnp.where(even, high, low)
        up_send[v, :, :width] = jnp.where(even, low, high)
        up_send[v, :, width:] = cols[v]
    top[...] = jnp.broadcast_to(largest.reshape(1, 1, 1), top.shape)


def shift_kernel(shift, came, sent, layer, out):
    radial, width = layer.shape[1], layer.shape[2]
    row = lax.axis_index("row")
    amount = shift[0] % width
    amount = jnp.where(row == 1, amount, jnp.where(row == 2, width - amount, 0))
    tiles = amount // LANES
    rest = amount % LANES
    lane = lax.broadcasted_iota(jnp.int32, (radial, LANES), 1)
    for v in range(6):
        parts = [
            pltpu.roll(ref[v, :, h * LANES : (h + 1) * LANES], rest, 1)
            for ref in (came, sent)
            for h in range(2)
        ]
        for t in range(2):
            picks = [
                jnp.where(lane < rest, parts[max(1 + t - q, 0)], parts[2 + t - q]) for q in range(3)
            ]
            out[v, :radial, t * LANES : (t + 1) * LANES] = jnp.where(
                tiles == 0, picks[0], jnp.where(tiles == 1, picks[1], picks[2])
            )
        out[v, radial:, :] = layer[v]


def weight_kernel(fwd, back, own, other, out):
    radial = out.shape[1]
    low = lax.axis_index("rad") == 0
    table = jnp.where(lax.axis_index("row") == 1, fwd[...], back[...])
    for v in range(6):
        mine, theirs = own[v, :radial], other[v, :radial]
        plane = jnp.concatenate([jnp.where(low, mine, theirs), jnp.where(low, theirs, mine)], 0)
        out[v] = jnp.dot(
            table, plane, precision=lax.Precision.HIGHEST, preferred_element_type=F32
        )


def closure(rho, nut, dist, grad2):
    square = jnp.maximum(grad2, GRAD_FLOOR * GRAD_FLOOR)
    inverse = lax.rsqrt(square)
    strain = square * inverse
    eight = (8.0 / (KAPPA * KAPPA)) * (nut + NU_LAM) * inverse / (dist * dist)
    shielding = 1.0 - jnp.tanh(eight * eight * eight)
    length = dist - shielding * jnp.maximum(0.0, dist - C_DES)
    quot = nut / length
    return shielding, rho * (CB1 * strain * nut - CW1 * (quot * quot))


def state_at(prim, der, a):
    return dict(
        rho=prim[0, a],
        u=[prim[1 + i, a] for i in range(3)],
        p=prim[4, a],
        m=[der[i, a] for i in range(3)],
        e=der[3, a],
        n=der[4, a],
        c=der[5, a],
    )


def face_kernel(
    prim, wall_in, core, layer, own_layer, wall_layer, came, col_next,
    col_own, top, flow_out, shield_out, edge_out,
    der, wall, flow, shield,
    low_face, lay_hi, lay_lo, lay_u, azi_hi, azi_lo, azi_u, sems, out_sems,
):
    _, count, radial, width = prim.shape
    row, rad = lax.axis_index("row"), lax.axis_index("rad")
    even = row % 2 == 0
    at_low = rad == 0
    parts = count // CHUNK

    def part_of(k):
        rows = pl.ds(k * CHUNK, CHUNK)
        return [pltpu.make_async_copy(wall_in.at[rows], wall.at[rows], sems.at[k])]

    def results_of(k):
        rows = pl.ds(k * CHUNK, CHUNK)
        return [
            pltpu.make_async_copy(flow.at[:, rows], flow_out.at[:, rows], out_sems.at[k, 0]),
            pltpu.make_async_copy(shield.at[rows], shield_out.at[rows], out_sems.at[k, 1]),
        ]

    for k in range(parts):
        for c in part_of(k):
            c.start()
    step_size = CFL / jnp.max(top[...])
    half = 0.5 * step_size
    sub = lax.broadcasted_iota(jnp.int32, (8, width), 0)
    lane = lax.broadcasted_iota(jnp.int32, (radial, LANES), 1)

    def derive(a):
        q = [prim[v, a] for v in range(6)]
        s = state_of(q)
        for i in range(3):
            der[i, a] = s["m"][i]
        der[3, a] = s["e"]
        der[4, a] = s["n"]
        der[5, a] = s["c"]

    def up_r(v, halo):
        lo, hi = pltpu.roll(v[:8], 7, 0), pltpu.roll(v[8:], 7, 0)
        edge = sub == 7
        return jnp.concatenate([jnp.where(edge, hi, lo), jnp.where(edge, halo, hi)], 0)

    def down_r(v, halo):
        lo, hi = pltpu.roll(v[:8], 1, 0), pltpu.roll(v[8:], 1, 0)
        edge = sub == 0
        return jnp.concatenate([jnp.where(edge, halo, lo), jnp.where(edge, lo, hi)], 0)

    def up_t(v, halo):
        lo, hi = pltpu.roll(v[:, :LANES], LANES - 1, 1), pltpu.roll(v[:, LANES:], LANES - 1, 1)
        edge = lane == LANES - 1
        return jnp.concatenate([jnp.where(edge, hi, lo), jnp.where(edge, halo, hi)], 1)

    def down_t(v, halo):
        lo, hi = pltpu.roll(v[:, :LANES], 1, 1), pltpu.roll(v[:, LANES:], 1, 1)
        edge = lane == 0
        return jnp.concatenate([jnp.where(edge, halo, lo), jnp.where(edge, lo, hi)], 1)

    def mirrored(q):
        return [q[0], q[1], -q[2], q[3], q[4], q[5]]

    got = [layer[v, radial:] for v in range(6)]
    bottom = [jnp.where(at_low, wall_layer[v], own_layer[v]) for v in range(6)]
    ceiling = [jnp.where(at_low, own_layer[v], wall_layer[v]) for v in range(6)]
    high = [jnp.where(at_low, g, w) for g, w in zip(got, mirrored(ceiling))]
    low = [jnp.where(at_low, w, g) for g, w in zip(got, mirrored(bottom))]
    high_state = pack_state(state_of(high))
    for i, name in enumerate(PASSED):
        lay_hi[i] = high_state[name]
    for i, f in enumerate(face_of(state_of(low), state_of(bottom), 1)):
        lay_lo[i] = f
    for i in range(3):
        lay_u[i] = low[1 + i]

    def column(ref, v):
        q = ref[v, :, ref.shape[2] - LANES :]
        return jnp.where(lane < 2 * count, q, 1.0)

    nxt_state = pack_state(state_of([column(col_next, v) for v in range(6)]))
    for i, name in enumerate(PASSED):
        azi_hi[i] = nxt_state[name]
    prev = [column(came, v) for v in range(6)]
    for i, f in enumerate(face_of(state_of(prev), state_of([pltpu.roll(column(col_own, v), LANES - 1, 1) for v in range(6)]), 2)):
        azi_lo[i] = f
    for i in range(3):
        azi_u[i] = prev[1 + i]

    end = [core[v] for v in range(6)]
    end_state = state_of(end)
    no_low = jnp.where(even, 0.0, 1.0)
    no_high = jnp.where(even, 1.0, 0.0)
    for c in part_of(0):
        c.wait()
    derive(0)
    for i, f in enumerate(face_of(end_state, state_at(prim, der, 0), 0)):
        low_face[i] = f * no_low

    def step(a, _):
        here = state_at(prim, der, a)
        last = a == count - 1
        first = a == 0
        later = jnp.minimum(a + 1, count - 1)
        earlier = jnp.maximum(a - 1, 0)
        total = [None] * 6
        derive(later)
        above = state_at(prim, der, later)
        right = dict(
            (k, [jnp.where(last, g, h) for g, h in zip(end_state[k], above[k])])
            if isinstance(above[k], list)
            else (k, jnp.where(last, end_state[k], above[k]))
            for k in above
        )
        keep = jnp.where(last, no_high, 1.0)
        for i, f in enumerate(face_of(here, right, 0)):
            f = f * keep
            total[i] = f - low_face[i]
            low_face[i] = f
        grad2 = None
        for i in range(3):
            down = jnp.where(first, end[1 + i], prim[1 + i, earlier])
            d = right["u"][i] - down
            grad2 = d * d if grad2 is None else grad2 + d * d
        outermost = jnp.where(even, first, last)
        grad2 = grad2 * jnp.where(outermost, 0.0, 1.0)
        packed = pack_state(here)
        row_of = pl.ds(a, 1)
        shifted = {n: up_r(packed[n], lay_hi[i, row_of, :]) for i, n in enumerate(PASSED)}
        face = face_of(here, unpack_state(shifted), 1)
        for i, f in enumerate(face):
            total[i] = total[i] + (f - down_r(f, lay_lo[i, row_of, :]))
        for i in range(3):
            d = shifted["u%d" % i] - down_r(here["u"][i], lay_u[i, row_of, :])
            grad2 = grad2 + d * d
        to_end = (LANES - 2) - 2 * a
        to_start = (LANES - 2 * a) % LANES
        shifted = {n: up_t(packed[n], pltpu.roll(azi_hi[i], to_end, 1)) for i, n in enumerate(PASSED)}
        face = face_of(here, unpack_state(shifted), 2)
        for i, f in enumerate(face):
            total[i] = total[i] + (f - down_t(f, pltpu.roll(azi_lo[i], to_start, 1)))
        for i in range(3):
            d = shifted["u%d" % i] - down_t(here["u"][i], pltpu.roll(azi_u[i], to_start, 1))
            grad2 = grad2 + d * d
        shielding, source = closure(here["rho"], prim[5, a], wall[a], 0.25 * grad2)
        cons = cons_of(here)
        for i in range(5):
            flow[i, a] = cons[i] - half * total[i]
        flow[5, a] = cons[5] - half * total[5] + step_size * source
        shield[a] = shielding

        @pl.when(outermost)
        def _():
            for i in range(6):
                edge_out[i] = cons[i] - half * total[i]
            edge_out[6] = grad2
            edge_out[7] = wall[a]
            inside = jnp.where(even, 1, count - 2)
            for i in range(3):
                edge_out[8 + i] = prim[1 + i, inside]
            edge_out[11] = jnp.zeros((radial, width), F32) + step_size

        return 0

    def part_step(k, _):
        @pl.when(k + 1 < parts)
        def _():
            for c in part_of(k + 1):
                c.wait()

        lax.fori_loop(k * CHUNK, (k + 1) * CHUNK, step, 0)
        for c in results_of(k):
            c.start()
        return 0

    lax.fori_loop(0, parts, part_step, 0)
    for k in range(parts):
        for c in results_of(k):
            c.wait()


def edge_kernel(
    flow_in, shield_in, edge, sent, ghost, flow_out, shield_out, edge_flow, edge_shield, sems
):
    del flow_in, shield_in
    _, radial, width = ghost.shape
    count = shield_out.shape[0]
    row = lax.axis_index("row")
    even = row % 2 == 0
    coupled = (row == 1) | (row == 2)
    end = jnp.where(even, 0, count - 1)
    step_size = edge[11]
    mine = [sent[v, :, :width] for v in range(6)]
    beyond = [jnp.where(coupled, ghost[v], mine[v]) for v in range(6)]
    here, out_state = state_of(mine), ghost_state_of(beyond)
    grad2 = 0.25 * edge[6]
    for i in range(3):
        d = 0.5 * (edge[8 + i] - beyond[1 + i])
        grad2 = grad2 + d * d

    def pick(p, q):
        return dict(
            (k, [jnp.where(even, x, y) for x, y in zip(p[k], q[k])])
            if isinstance(p[k], list)
            else (k, jnp.where(even, p[k], q[k]))
            for k in p
        )

    shielding, source = closure(here["rho"], mine[5], edge[7], grad2)
    edge_shield[...] = shielding
    sign = jnp.where(even, -1.0, 1.0)
    for i, f in enumerate(ghost_face_of(pick(out_state, here), pick(here, out_state), 0)):
        value = edge[i] - step_size * (sign * f)
        edge_flow[i] = value + step_size * source if i == 5 else value
    copies = [
        pltpu.make_async_copy(edge_flow, flow_out.at[:, end], sems.at[0]),
        pltpu.make_async_copy(edge_shield, shield_out.at[end], sems.at[1]),
    ]
    for c in copies:
        c.start()
    for c in copies:
        c.wait()


def derive_call(fields, devices):
    count, radial, width = fields[0].shape
    plane, layer = shaped(6, radial, width), shaped(6, count, width)
    return pl.pallas_call(
        derive_kernel,
        out_shape=(
            plane, shaped(6, radial, width + LANES), layer, layer, shaped(6, radial, LANES),
            shaped(devices, 1, LANES), pltpu.VMEM((6, count, radial, width), F32),
        ),
        in_specs=[HBM] * 4,
        out_specs=(VMEM,) * 7,
        scratch_shapes=[pltpu.SemaphoreType.DMA((count // CHUNK, 4))],
        compiler_params=params(),
        name="derive",
    )(*fields)


def faces_call(*arrays):
    whole = arrays[0].shape
    _, count, radial, width = whole
    parts = count // CHUNK
    return pl.pallas_call(
        face_kernel,
        out_shape=(apart(*whole), apart(count, radial, width), shaped(12, radial, width)),
        in_specs=[VMEM, HBM] + [VMEM] * 8,
        out_specs=(HBM, HBM, VMEM),
        scratch_shapes=[
            pltpu.VMEM(whole, F32),
            pltpu.VMEM((count, radial, width), F32),
            pltpu.VMEM(whole, F32),
            pltpu.VMEM((count, radial, width), F32),
            pltpu.VMEM((6, radial, width), F32),
            pltpu.VMEM((8, count, width), F32),
            pltpu.VMEM((6, count, width), F32),
            pltpu.VMEM((3, count, width), F32),
            pltpu.VMEM((8, radial, LANES), F32),
            pltpu.VMEM((6, radial, LANES), F32),
            pltpu.VMEM((3, radial, LANES), F32),
            pltpu.SemaphoreType.DMA((parts,)),
            pltpu.SemaphoreType.DMA((parts, 2)),
        ],
        compiler_params=params(),
        cost_estimate=pl.CostEstimate(
            flops=25_000_000, bytes_accessed=6_000_000, transcendentals=300_000
        ),
        name="faces",
    )(*arrays)


def edge_call(flow, shield, edge, sent, ghost):
    _, radial, width = ghost.shape
    return pl.pallas_call(
        edge_kernel,
        out_shape=(shaped(*flow.shape), shaped(*shield.shape)),
        in_specs=[HBM] * 2 + [VMEM] * 3,
        out_specs=(HBM, HBM),
        input_output_aliases={0: 0, 1: 1},
        scratch_shapes=[
            pltpu.VMEM((6, radial, width), F32),
            pltpu.VMEM((radial, width), F32),
            pltpu.SemaphoreType.DMA((2,)),
        ],
        compiler_params=params(),
        name="edge",
    )(flow, shield, edge, sent, ghost)


def body(density, velocity, pressure, nu_tilde, wall_distance, interp_fwd, interp_back, offset):
    rows, rads, cycle = (lax.axis_size(n) for n in AXES)
    count, radial, width = density.shape

    def device(row, rad, azi):
        return (row * rads + rad) * cycle + azi % cycle

    def everyone(target):
        return [
            (device(r, d, a), target(r, d, a))
            for r in range(rows)
            for d in range(rads)
            for a in range(cycle)
        ]

    plane = shaped(6, radial, width)
    devices = rows * rads * cycle
    fields = [far_away(x) for x in (density, velocity, pressure, nu_tilde)]
    core, up_send, layer, far_layer, cols, top, prim = derive_call(fields, devices)

    up = everyone(lambda r, d, a: device(r, d, a + 1))
    down = everyone(lambda r, d, a: device(r, d, a - 1))
    pair = everyone(lambda r, d, a: device(r ^ 1, d, a))
    across = everyone(lambda r, d, a: device(r, rads - 1 - d, a))
    tops = lax.all_to_all(top, AXES, 0, 0)
    came = lax.ppermute(up_send, AXES, up)
    col_next = lax.ppermute(cols, AXES, down)
    core_got = lax.ppermute(core, AXES, pair)

    moved = pl.pallas_call(
        shift_kernel,
        out_shape=shaped(6, radial + count, width),
        in_specs=[SMEM, VMEM, VMEM, VMEM],
        out_specs=VMEM,
        compiler_params=params(),
        name="shift",
    )(offset, came, up_send, layer)
    swapped = lax.ppermute(moved, AXES, across)
    weighted = pl.pallas_call(
        weight_kernel,
        out_shape=plane,
        in_specs=[VMEM] * 4,
        out_specs=VMEM,
        compiler_params=params(),
        name="weigh",
    )(interp_fwd, interp_back, moved, swapped)

    def far(blocks):
        route = []
        for d in range(rads):
            for a in range(cycle):
                route.append((device(1, d, a), device(2, d, a + blocks)))
                route.append((device(2, d, a), device(1, d, a + cycle - 1 - blocks)))

        def branch(block, sent, near, dist, *rest):
            near = pltpu.with_memory_space_constraint(near, pltpu.VMEM)
            ghost = lax.ppermute(block, AXES, route)
            flow, shield, edge = faces_call(near, far_away(dist), *rest)
            return edge_call(far_away(flow), far_away(shield), edge, sent, ghost)

        return branch

    return lax.switch(
        offset[0] // width,
        [far(b) for b in range(cycle)],
        weighted, up_send, prim, wall_distance,
        core_got, swapped, layer, far_layer, came, col_next, cols, tops,
    )


def solution(mesh):
    placed = (
        P("row", "rad", "azi"),
        P(None, "row", "rad", "azi"),
        P("row", "rad", "azi"),
        P("row", "rad", "azi"),
        P("row", "rad", "azi"),
        P("rad", None),
        P("rad", None),
        P(),
    )
    return jax.shard_map(
        body,
        mesh=mesh,
        in_specs=placed,
        out_specs=(P(None, "row", "rad", "azi"), P("row", "rad", "azi")),
        check_vma=False,
    )
```

```python
import functools

import jax
import jax.numpy as jnp
from jax import lax
from jax.experimental import pallas as pl
from jax.experimental.pallas import tpu as pltpu
from jax.sharding import PartitionSpec as P

GAMMA = 1.4
CFL = 0.8
KAPPA = 0.41
C_DES = 0.65
CB1 = 0.1355
CW1 = 3.239
NU_LAM = 0.001
GRAD_FLOOR = 0.2

AXES = ("row", "rad", "azi")
LANES = 128
CHUNK = 4
FIRST_CHUNK = 8
F32 = jnp.float32
VMEM = pl.BlockSpec(memory_space=pltpu.VMEM)
SMEM = pl.BlockSpec(memory_space=pltpu.SMEM)
HBM = pl.BlockSpec(memory_space=pltpu.HBM)


def params(mib=32):
    return pltpu.CompilerParams(vmem_limit_bytes=mib * 1024 * 1024)


def shaped(*dims):
    return jax.ShapeDtypeStruct(dims, F32)


def apart(*dims):
    return pltpu.HBM(dims, F32)


def far_away(array):
    return pltpu.with_memory_space_constraint(array, pltpu.HBM)


def sound_speed(rho, press):
    scaled = GAMMA * press
    return scaled * lax.rsqrt(scaled * rho)


def energy_of(press, m, u):
    return press * (1.0 / (GAMMA - 1.0)) + 0.5 * (m[0] * u[0] + m[1] * u[1] + m[2] * u[2])


def state_of(prim):
    rho, u, press, nut = prim[0], prim[1:4], prim[4], prim[5]
    m = [rho * v for v in u]
    return dict(
        rho=rho, m=m, u=u, p=press, e=energy_of(press, m, u), n=rho * nut, c=sound_speed(rho, press)
    )


def ghost_state_of(prim):
    rho, u, press, nut = prim[0], prim[1:4], prim[4], prim[5]
    kinetic = 0.5 * rho * (u[0] * u[0] + u[1] * u[1] + u[2] * u[2])
    return dict(
        rho=rho, m=[rho * v for v in u], u=u, p=press, e=press / (GAMMA - 1.0) + kinetic, n=rho * nut,
        c=jnp.sqrt(GAMMA * press / rho),
    )


def cons_of(s):
    return [s["rho"], s["m"][0], s["m"][1], s["m"][2], s["e"], s["n"]]


def flux_of(s, k):
    w = s["u"][k]
    mom = [s["m"][k] * s["u"][i] for i in range(3)]
    mom[k] = mom[k] + s["p"]
    return [s["m"][k], mom[0], mom[1], mom[2], (s["e"] + s["p"]) * w, s["n"] * w]


def face_of(left, right, k):
    wave = jnp.maximum(jnp.abs(left["u"][k]) + left["c"], jnp.abs(right["u"][k]) + right["c"])
    return [
        (fl + fr) - wave * (ur - ul)
        for fl, fr, ul, ur in zip(
            flux_of(left, k), flux_of(right, k), cons_of(left), cons_of(right)
        )
    ]


def ghost_face_of(left, right, k):
    wave = jnp.maximum(jnp.abs(left["u"][k]) + left["c"], jnp.abs(right["u"][k]) + right["c"])
    return [
        0.5 * (fl + fr) - 0.5 * wave * (ur - ul)
        for fl, fr, ul, ur in zip(
            flux_of(left, k), flux_of(right, k), cons_of(left), cons_of(right)
        )
    ]


NAMES = ("rho", "u0", "u1", "u2", "p", "m0", "m1", "m2", "e", "n", "c")
PASSED = ("rho", "u0", "u1", "u2", "p", "e", "n", "c")


def pack_state(s):
    return dict(
        rho=s["rho"], u0=s["u"][0], u1=s["u"][1], u2=s["u"][2], p=s["p"], e=s["e"], n=s["n"], c=s["c"]
    )


def unpack_state(d):
    u = [d["u0"], d["u1"], d["u2"]]
    return dict(rho=d["rho"], u=u, m=[d["rho"] * v for v in u], p=d["p"], e=d["e"], n=d["n"], c=d["c"])


def fetch(sources, prim, rows, sems):
    rho, vel, press, nut = sources
    return [
        pltpu.make_async_copy(rho.at[rows], prim.at[0, rows], sems.at[0]),
        pltpu.make_async_copy(vel.at[:, rows], prim.at[pl.ds(1, 3), rows], sems.at[1]),
        pltpu.make_async_copy(press.at[rows], prim.at[4, rows], sems.at[2]),
        pltpu.make_async_copy(nut.at[rows], prim.at[5, rows], sems.at[3]),
    ]


def derive_kernel(
    rho_in, vel_in, press_in, nut_in, core, up_send, layer, far_layer, cols, top, prim, sems,
):
    _, count, radial, width = prim.shape
    even = lax.axis_index("row") % 2 == 0
    inner_rad = lax.axis_index("rad") == 0
    lane = lax.broadcasted_iota(jnp.int32, (radial, LANES), 1)
    parts = count // FIRST_CHUNK

    def part_of(k):
        return fetch((rho_in, vel_in, press_in, nut_in), prim, pl.ds(k * FIRST_CHUNK, FIRST_CHUNK), sems.at[k])

    for k in range(parts):
        for c in part_of(k):
            c.start()
    cols[...] = jnp.zeros(cols.shape, F32)

    def step(a, best):
        speed = 3.0 * sound_speed(prim[0, a], prim[4, a])
        here = lane // 2 == a
        for v in range(6):
            plane = prim[v, a]
            if 1 <= v <= 3:
                speed = speed + jnp.abs(plane)
            high, low = plane[radial - 1 :], plane[:1]
            layer[v, pl.ds(a, 1), :] = jnp.where(inner_rad, high, low)
            far_layer[v, pl.ds(a, 1), :] = jnp.where(inner_rad, low, high)
            first, last = plane[:, :LANES], plane[:, width - LANES :]
            both = pltpu.roll(jnp.where(lane == 0, first, last), 2 * a + 1, 1)
            cols[v] = jnp.where(here, both, cols[v])
        return jnp.maximum(best, speed)

    best = jnp.zeros((radial, width), F32)
    for k in range(parts):
        for c in part_of(k):
            c.wait()
        for j in range(FIRST_CHUNK):
            best = step(k * FIRST_CHUNK + j, best)
    largest = jnp.max(best, axis=0, keepdims=True)
    largest = jnp.max(largest, axis=1, keepdims=True)
    for v in range(6):
        low, high = prim[v, 0], prim[v, count - 1]
        core[v] = jnp.where(even, high, low)
        up_send[v, :, :width] = jnp.where(even, low, high)
        up_send[v, :, width:] = cols[v]
    top[...] = jnp.broadcast_to(largest.reshape(1, 1, 1), top.shape)


def shift_kernel(shift, came, sent, layer, out):
    radial, width = layer.shape[1], layer.shape[2]
    row = lax.axis_index("row")
    amount = shift[0] % width
    amount = jnp.where(row == 1, amount, jnp.where(row == 2, width - amount, 0))
    tiles = amount // LANES
    rest = amount % LANES
    lane = lax.broadcasted_iota(jnp.int32, (radial, LANES), 1)
    for v in range(6):
        parts = [
            pltpu.roll(ref[v, :, h * LANES : (h + 1) * LANES], rest, 1)
            for ref in (came, sent)
            for h in range(2)
        ]
        for t in range(2):
            picks = [
                jnp.where(lane < rest, parts[max(1 + t - q, 0)], parts[2 + t - q]) for q in range(3)
            ]
            out[v, :radial, t * LANES : (t + 1) * LANES] = jnp.where(
                tiles == 0, picks[0], jnp.where(tiles == 1, picks[1], picks[2])
            )
        out[v, radial:, :] = layer[v]


def weight_kernel(fwd, back, own, other, out):
    radial = out.shape[1]
    low = lax.axis_index("rad") == 0
    table = jnp.where(lax.axis_index("row") == 1, fwd[...], back[...])
    for v in range(6):
        mine, theirs = own[v, :radial], other[v, :radial]
        plane = jnp.concatenate([jnp.where(low, mine, theirs), jnp.where(low, theirs, mine)], 0)
        out[v] = jnp.dot(
            table, plane, precision=lax.Precision.HIGHEST, preferred_element_type=F32
        )


def closure(rho, nut, dist, grad2):
    square = jnp.maximum(grad2, GRAD_FLOOR * GRAD_FLOOR)
    inverse = lax.rsqrt(square)
    strain = square * inverse
    eight = (8.0 / (KAPPA * KAPPA)) * (nut + NU_LAM) * inverse / (dist * dist)
    shielding = 1.0 - jnp.tanh(eight * eight * eight)
    length = dist - shielding * jnp.maximum(0.0, dist - C_DES)
    quot = nut / length
    return shielding, rho * (CB1 * strain * nut - CW1 * (quot * quot))


def state_at(prim, der, a):
    return dict(
        rho=prim[0, a],
        u=[prim[1 + i, a] for i in range(3)],
        p=prim[4, a],
        m=[der[i, a] for i in range(3)],
        e=der[3, a],
        n=der[4, a],
        c=der[5, a],
    )


def face_kernel(
    prim, wall_in, core, layer, own_layer, wall_layer, came, col_next,
    col_own, top, flow_out, shield_out, edge_out, tail_out,
    der, wall, flow, shield,
    low_face, lay_hi, lay_lo, lay_u, azi_hi, azi_lo, azi_u, sems, out_sems,
):
    _, count, radial, width = prim.shape
    row, rad = lax.axis_index("row"), lax.axis_index("rad")
    even = row % 2 == 0
    at_low = rad == 0
    parts = count // CHUNK

    def part_of(k):
        rows = pl.ds(k * CHUNK, CHUNK)
        return [pltpu.make_async_copy(wall_in.at[rows], wall.at[rows], sems.at[k])]

    def results_of(k):
        rows = pl.ds(k * CHUNK, CHUNK)
        return [
            pltpu.make_async_copy(flow.at[:, rows], flow_out.at[:, rows], out_sems.at[k, 0]),
            pltpu.make_async_copy(shield.at[rows], shield_out.at[rows], out_sems.at[k, 1]),
        ]

    for k in range(parts):
        for c in part_of(k):
            c.start()
    step_size = CFL / jnp.max(top[...])
    half = 0.5 * step_size
    sub = lax.broadcasted_iota(jnp.int32, (8, width), 0)
    lane = lax.broadcasted_iota(jnp.int32, (radial, LANES), 1)

    def derive(a):
        q = [prim[v, a] for v in range(6)]
        s = state_of(q)
        for i in range(3):
            der[i, a] = s["m"][i]
        der[3, a] = s["e"]
        der[4, a] = s["n"]
        der[5, a] = s["c"]

    def up_r(v, halo):
        lo, hi = pltpu.roll(v[:8], 7, 0), pltpu.roll(v[8:], 7, 0)
        edge = sub == 7
        return jnp.concatenate([jnp.where(edge, hi, lo), jnp.where(edge, halo, hi)], 0)

    def down_r(v, halo):
        lo, hi = pltpu.roll(v[:8], 1, 0), pltpu.roll(v[8:], 1, 0)
        edge = sub == 0
        return jnp.concatenate([jnp.where(edge, halo, lo), jnp.where(edge, lo, hi)], 0)

    def up_t(v, halo):
        lo, hi = pltpu.roll(v[:, :LANES], LANES - 1, 1), pltpu.roll(v[:, LANES:], LANES - 1, 1)
        edge = lane == LANES - 1
        return jnp.concatenate([jnp.where(edge, hi, lo), jnp.where(edge, halo, hi)], 1)

    def down_t(v, halo):
        lo, hi = pltpu.roll(v[:, :LANES], 1, 1), pltpu.roll(v[:, LANES:], 1, 1)
        edge = lane == 0
        return jnp.concatenate([jnp.where(edge, halo, lo), jnp.where(edge, lo, hi)], 1)

    def mirrored(q):
        return [q[0], q[1], -q[2], q[3], q[4], q[5]]

    got = [layer[v, radial:] for v in range(6)]
    bottom = [jnp.where(at_low, wall_layer[v], own_layer[v]) for v in range(6)]
    ceiling = [jnp.where(at_low, own_layer[v], wall_layer[v]) for v in range(6)]
    high = [jnp.where(at_low, g, w) for g, w in zip(got, mirrored(ceiling))]
    low = [jnp.where(at_low, w, g) for g, w in zip(got, mirrored(bottom))]
    high_state = pack_state(state_of(high))
    for i, name in enumerate(PASSED):
        lay_hi[i] = high_state[name]
    for i, f in enumerate(face_of(state_of(low), state_of(bottom), 1)):
        lay_lo[i] = f
    for i in range(3):
        lay_u[i] = low[1 + i]

    def column(ref, v):
        q = ref[v, :, ref.shape[2] - LANES :]
        return jnp.where(lane < 2 * count, q, 1.0)

    nxt_state = pack_state(state_of([column(col_next, v) for v in range(6)]))
    for i, name in enumerate(PASSED):
        azi_hi[i] = nxt_state[name]
    prev = [column(came, v) for v in range(6)]
    for i, f in enumerate(face_of(state_of(prev), state_of([pltpu.roll(column(col_own, v), LANES - 1, 1) for v in range(6)]), 2)):
        azi_lo[i] = f
    for i in range(3):
        azi_u[i] = prev[1 + i]

    end = [core[v] for v in range(6)]
    end_state = state_of(end)
    no_low = jnp.where(even, 0.0, 1.0)
    no_high = jnp.where(even, 1.0, 0.0)
    for c in part_of(0):
        c.wait()
    derive(0)
    for i, f in enumerate(face_of(end_state, state_at(prim, der, 0), 0)):
        low_face[i] = f * no_low

    def step(a, _):
        here = state_at(prim, der, a)
        last = a == count - 1
        first = a == 0
        later = jnp.minimum(a + 1, count - 1)
        earlier = jnp.maximum(a - 1, 0)
        total = [None] * 6
        derive(later)
        above = state_at(prim, der, later)
        right = dict(
            (k, [jnp.where(last, g, h) for g, h in zip(end_state[k], above[k])])
            if isinstance(above[k], list)
            else (k, jnp.where(last, end_state[k], above[k]))
            for k in above
        )
        keep = jnp.where(last, no_high, 1.0)
        for i, f in enumerate(face_of(here, right, 0)):
            f = f * keep
            total[i] = f - low_face[i]
            low_face[i] = f
        grad2 = None
        for i in range(3):
            down = jnp.where(first, end[1 + i], prim[1 + i, earlier])
            d = right["u"][i] - down
            grad2 = d * d if grad2 is None else grad2 + d * d
        outermost = jnp.where(even, first, last)
        grad2 = grad2 * jnp.where(outermost, 0.0, 1.0)
        packed = pack_state(here)
        row_of = pl.ds(a, 1)
        shifted = {n: up_r(packed[n], lay_hi[i, row_of, :]) for i, n in enumerate(PASSED)}
        face = face_of(here, unpack_state(shifted), 1)
        for i, f in enumerate(face):
            total[i] = total[i] + (f - down_r(f, lay_lo[i, row_of, :]))
        for i in range(3):
            d = shifted["u%d" % i] - down_r(here["u"][i], lay_u[i, row_of, :])
            grad2 = grad2 + d * d
        to_end = (LANES - 2) - 2 * a
        to_start = (LANES - 2 * a) % LANES
        shifted = {n: up_t(packed[n], pltpu.roll(azi_hi[i], to_end, 1)) for i, n in enumerate(PASSED)}
        face = face_of(here, unpack_state(shifted), 2)
        for i, f in enumerate(face):
            total[i] = total[i] + (f - down_t(f, pltpu.roll(azi_lo[i], to_start, 1)))
        for i in range(3):
            d = shifted["u%d" % i] - down_t(here["u"][i], pltpu.roll(azi_u[i], to_start, 1))
            grad2 = grad2 + d * d
        shielding, source = closure(here["rho"], prim[5, a], wall[a], 0.25 * grad2)
        cons = cons_of(here)
        for i in range(5):
            flow[i, a] = cons[i] - half * total[i]
        flow[5, a] = cons[5] - half * total[5] + step_size * source
        shield[a] = shielding

        @pl.when(outermost)
        def _():
            for i in range(6):
                edge_out[i] = cons[i] - half * total[i]
            edge_out[6] = grad2
            edge_out[7] = wall[a]
            inside = jnp.where(even, 1, count - 2)
            for i in range(3):
                edge_out[8 + i] = prim[1 + i, inside]
            edge_out[11] = jnp.zeros((radial, width), F32) + step_size

        return 0

    def part_step(k, _):
        @pl.when(k + 1 < parts)
        def _():
            for c in part_of(k + 1):
                c.wait()

        lax.fori_loop(k * CHUNK, (k + 1) * CHUNK, step, 0)
        @pl.when(k + 1 < parts)
        def _():
            for c in results_of(k):
                c.start()

        return 0

    lax.fori_loop(0, parts, part_step, 0)
    for j in range(CHUNK):
        for i in range(6):
            tail_out[i, j] = flow[i, count - CHUNK + j]
        tail_out[6, j] = shield[count - CHUNK + j]
    for k in range(parts - 1):
        for c in results_of(k):
            c.wait()


def edge_kernel(
    flow_in, shield_in, edge, tail, sent, ghost, flow_out, shield_out,
    edge_flow, edge_shield, last_flow, last_shield, sems,
):
    del flow_in, shield_in
    _, radial, width = ghost.shape
    count = shield_out.shape[0]
    row = lax.axis_index("row")
    even = row % 2 == 0
    coupled = (row == 1) | (row == 2)
    step_size = edge[11]
    rows = pl.ds(count - CHUNK, CHUNK - 1)
    copies = [
        pltpu.make_async_copy(
            tail.at[pl.ds(0, 6), pl.ds(0, CHUNK - 1)], flow_out.at[:, rows], sems.at[0]
        ),
        pltpu.make_async_copy(tail.at[6, pl.ds(0, CHUNK - 1)], shield_out.at[rows], sems.at[1]),
    ]
    for c in copies:
        c.start()
    mine = [sent[v, :, :width] for v in range(6)]
    beyond = [jnp.where(coupled, ghost[v], mine[v]) for v in range(6)]
    here, out_state = state_of(mine), ghost_state_of(beyond)
    grad2 = 0.25 * edge[6]
    for i in range(3):
        d = 0.5 * (edge[8 + i] - beyond[1 + i])
        grad2 = grad2 + d * d

    def pick(p, q):
        return dict(
            (k, [jnp.where(even, x, y) for x, y in zip(p[k], q[k])])
            if isinstance(p[k], list)
            else (k, jnp.where(even, p[k], q[k]))
            for k in p
        )

    shielding, source = closure(here["rho"], mine[5], edge[7], grad2)
    edge_shield[...] = shielding
    last_shield[...] = jnp.where(even, tail[6, CHUNK - 1], shielding)
    sign = jnp.where(even, -1.0, 1.0)
    for i, f in enumerate(ghost_face_of(pick(out_state, here), pick(here, out_state), 0)):
        value = edge[i] - step_size * (sign * f)
        if i == 5:
            value = value + step_size * source
        edge_flow[i] = value
        last_flow[i] = jnp.where(even, tail[i, CHUNK - 1], value)
    copies += [
        pltpu.make_async_copy(last_flow, flow_out.at[:, count - 1], sems.at[2]),
        pltpu.make_async_copy(last_shield, shield_out.at[count - 1], sems.at[3]),
    ]
    firsts = [
        pltpu.make_async_copy(edge_flow, flow_out.at[:, 0], sems.at[4]),
        pltpu.make_async_copy(edge_shield, shield_out.at[0], sems.at[5]),
    ]
    for c in copies[2:]:
        c.start()

    @pl.when(even)
    def _():
        for c in firsts:
            c.start()
        for c in firsts:
            c.wait()

    for c in copies:
        c.wait()


def derive_call(fields, devices):
    count, radial, width = fields[0].shape
    plane, layer = shaped(6, radial, width), shaped(6, count, width)
    return pl.pallas_call(
        derive_kernel,
        out_shape=(
            plane, shaped(6, radial, width + LANES), layer, layer, shaped(6, radial, LANES),
            shaped(devices, 1, LANES), pltpu.VMEM((6, count, radial, width), F32),
        ),
        in_specs=[HBM] * 4,
        out_specs=(VMEM,) * 7,
        scratch_shapes=[pltpu.SemaphoreType.DMA((count // FIRST_CHUNK, 4))],
        compiler_params=params(),
        name="derive",
    )(*fields)


def faces_call(*arrays):
    whole = arrays[0].shape
    _, count, radial, width = whole
    parts = count // CHUNK
    return pl.pallas_call(
        face_kernel,
        out_shape=(
            apart(*whole), apart(count, radial, width), shaped(12, radial, width),
            shaped(7, CHUNK, radial, width),
        ),
        in_specs=[VMEM, HBM] + [VMEM] * 8,
        out_specs=(HBM, HBM, VMEM, VMEM),
        scratch_shapes=[
            pltpu.VMEM(whole, F32),
            pltpu.VMEM((count, radial, width), F32),
            pltpu.VMEM(whole, F32),
            pltpu.VMEM((count, radial, width), F32),
            pltpu.VMEM((6, radial, width), F32),
            pltpu.VMEM((8, count, width), F32),
            pltpu.VMEM((6, count, width), F32),
            pltpu.VMEM((3, count, width), F32),
            pltpu.VMEM((8, radial, LANES), F32),
            pltpu.VMEM((6, radial, LANES), F32),
            pltpu.VMEM((3, radial, LANES), F32),
            pltpu.SemaphoreType.DMA((parts,)),
            pltpu.SemaphoreType.DMA((parts, 2)),
        ],
        compiler_params=params(),
        cost_estimate=pl.CostEstimate(
            flops=25_000_000, bytes_accessed=6_000_000, transcendentals=300_000
        ),
        name="faces",
    )(*arrays)


def edge_call(flow, shield, edge, tail, sent, ghost):
    _, radial, width = ghost.shape
    return pl.pallas_call(
        edge_kernel,
        out_shape=(shaped(*flow.shape), shaped(*shield.shape)),
        in_specs=[HBM] * 2 + [VMEM] * 4,
        out_specs=(HBM, HBM),
        input_output_aliases={0: 0, 1: 1},
        scratch_shapes=[
            pltpu.VMEM((6, radial, width), F32),
            pltpu.VMEM((radial, width), F32),
            pltpu.VMEM((6, radial, width), F32),
            pltpu.VMEM((radial, width), F32),
            pltpu.SemaphoreType.DMA((6,)),
        ],
        compiler_params=params(),
        name="edge",
    )(flow, shield, edge, tail, sent, ghost)


def body(density, velocity, pressure, nu_tilde, wall_distance, interp_fwd, interp_back, offset):
    rows, rads, cycle = (lax.axis_size(n) for n in AXES)
    count, radial, width = density.shape

    def device(row, rad, azi):
        return (row * rads + rad) * cycle + azi % cycle

    def everyone(target):
        return [
            (device(r, d, a), target(r, d, a))
            for r in range(rows)
            for d in range(rads)
            for a in range(cycle)
        ]

    plane = shaped(6, radial, width)
    devices = rows * rads * cycle
    fields = [far_away(x) for x in (density, velocity, pressure, nu_tilde)]
    core, up_send, layer, far_layer, cols, top, prim = derive_call(fields, devices)

    up = everyone(lambda r, d, a: device(r, d, a + 1))
    down = everyone(lambda r, d, a: device(r, d, a - 1))
    pair = everyone(lambda r, d, a: device(r ^ 1, d, a))
    across = everyone(lambda r, d, a: device(r, rads - 1 - d, a))
    tops = lax.all_to_all(top, AXES, 0, 0)
    came = lax.ppermute(up_send, AXES, up)
    col_next = lax.ppermute(cols, AXES, down)
    core_got = lax.ppermute(core, AXES, pair)

    moved = pl.pallas_call(
        shift_kernel,
        out_shape=shaped(6, radial + count, width),
        in_specs=[SMEM, VMEM, VMEM, VMEM],
        out_specs=VMEM,
        compiler_params=params(),
        name="shift",
    )(offset, came, up_send, layer)
    swapped = lax.ppermute(moved, AXES, across)
    weighted = pl.pallas_call(
        weight_kernel,
        out_shape=plane,
        in_specs=[VMEM] * 4,
        out_specs=VMEM,
        compiler_params=params(),
        name="weigh",
    )(interp_fwd, interp_back, moved, swapped)

    def far(blocks):
        route = []
        for d in range(rads):
            for a in range(cycle):
                route.append((device(1, d, a), device(2, d, a + blocks)))
                route.append((device(2, d, a), device(1, d, a + cycle - 1 - blocks)))

        def branch(block, sent, near, dist, *rest):
            near = pltpu.with_memory_space_constraint(near, pltpu.VMEM)
            ghost = lax.ppermute(block, AXES, route)
            flow, shield, edge, tail = faces_call(near, far_away(dist), *rest)
            return edge_call(far_away(flow), far_away(shield), edge, tail, sent, ghost)

        return branch

    return lax.switch(
        offset[0] // width,
        [far(b) for b in range(cycle)],
        weighted, up_send, prim, wall_distance,
        core_got, swapped, layer, far_layer, came, col_next, cols, tops,
    )


def solution(mesh):
    placed = (
        P("row", "rad", "azi"),
        P(None, "row", "rad", "azi"),
        P("row", "rad", "azi"),
        P("row", "rad", "azi"),
        P("row", "rad", "azi"),
        P("rad", None),
        P("rad", None),
        P(),
    )
    return jax.shard_map(
        body,
        mesh=mesh,
        in_specs=placed,
        out_specs=(P(None, "row", "rad", "azi"), P("row", "rad", "azi")),
        check_vma=False,
    )
```

```python
import functools

import jax
import jax.numpy as jnp
from jax import lax
from jax.experimental import pallas as pl
from jax.experimental.pallas import tpu as pltpu
from jax.sharding import PartitionSpec as P

GAMMA = 1.4
CFL = 0.8
KAPPA = 0.41
C_DES = 0.65
CB1 = 0.1355
CW1 = 3.239
NU_LAM = 0.001
GRAD_FLOOR = 0.2

AXES = ("row", "rad", "azi")
LANES = 128
CHUNK = 4
FIRST_CHUNK = 8
F32 = jnp.float32
VMEM = pl.BlockSpec(memory_space=pltpu.VMEM)
SMEM = pl.BlockSpec(memory_space=pltpu.SMEM)
HBM = pl.BlockSpec(memory_space=pltpu.HBM)


def params(mib=32):
    return pltpu.CompilerParams(vmem_limit_bytes=mib * 1024 * 1024)


def shaped(*dims):
    return jax.ShapeDtypeStruct(dims, F32)


def apart(*dims):
    return pltpu.HBM(dims, F32)


def far_away(array):
    return pltpu.with_memory_space_constraint(array, pltpu.HBM)


def sound_speed(rho, press):
    scaled = GAMMA * press
    return scaled * lax.rsqrt(scaled * rho)


def energy_of(press, m, u):
    return press * (1.0 / (GAMMA - 1.0)) + 0.5 * (m[0] * u[0] + m[1] * u[1] + m[2] * u[2])


def state_of(prim):
    rho, u, press, nut = prim[0], prim[1:4], prim[4], prim[5]
    m = [rho * v for v in u]
    return dict(
        rho=rho, m=m, u=u, p=press, e=energy_of(press, m, u), n=rho * nut, c=sound_speed(rho, press)
    )


def ghost_state_of(prim):
    rho, u, press, nut = prim[0], prim[1:4], prim[4], prim[5]
    kinetic = 0.5 * rho * (u[0] * u[0] + u[1] * u[1] + u[2] * u[2])
    return dict(
        rho=rho, m=[rho * v for v in u], u=u, p=press, e=press / (GAMMA - 1.0) + kinetic, n=rho * nut,
        c=jnp.sqrt(GAMMA * press / rho),
    )


def cons_of(s):
    return [s["rho"], s["m"][0], s["m"][1], s["m"][2], s["e"], s["n"]]


def flux_of(s, k):
    w = s["u"][k]
    mom = [s["m"][k] * s["u"][i] for i in range(3)]
    mom[k] = mom[k] + s["p"]
    return [s["m"][k], mom[0], mom[1], mom[2], (s["e"] + s["p"]) * w, s["n"] * w]


def face_of(left, right, k):
    wave = jnp.maximum(jnp.abs(left["u"][k]) + left["c"], jnp.abs(right["u"][k]) + right["c"])
    return [
        (fl + fr) - wave * (ur - ul)
        for fl, fr, ul, ur in zip(
            flux_of(left, k), flux_of(right, k), cons_of(left), cons_of(right)
        )
    ]


def ghost_face_of(left, right, k):
    wave = jnp.maximum(jnp.abs(left["u"][k]) + left["c"], jnp.abs(right["u"][k]) + right["c"])
    return [
        0.5 * (fl + fr) - 0.5 * wave * (ur - ul)
        for fl, fr, ul, ur in zip(
            flux_of(left, k), flux_of(right, k), cons_of(left), cons_of(right)
        )
    ]


NAMES = ("rho", "u0", "u1", "u2", "p", "m0", "m1", "m2", "e", "n", "c")
PASSED = ("rho", "u0", "u1", "u2", "p", "e", "n", "c")


def pack_state(s):
    return dict(
        rho=s["rho"], u0=s["u"][0], u1=s["u"][1], u2=s["u"][2], p=s["p"], e=s["e"], n=s["n"], c=s["c"]
    )


def unpack_state(d):
    u = [d["u0"], d["u1"], d["u2"]]
    return dict(rho=d["rho"], u=u, m=[d["rho"] * v for v in u], p=d["p"], e=d["e"], n=d["n"], c=d["c"])


def fetch(sources, prim, rows, sems):
    rho, vel, press, nut = sources
    return [
        pltpu.make_async_copy(rho.at[rows], prim.at[0, rows], sems.at[0]),
        pltpu.make_async_copy(vel.at[:, rows], prim.at[pl.ds(1, 3), rows], sems.at[1]),
        pltpu.make_async_copy(press.at[rows], prim.at[4, rows], sems.at[2]),
        pltpu.make_async_copy(nut.at[rows], prim.at[5, rows], sems.at[3]),
    ]


def derive_kernel(
    rho_in, vel_in, press_in, nut_in, core, up_send, layer, far_layer, cols, top, prim, sems,
):
    _, count, radial, width = prim.shape
    even = lax.axis_index("row") % 2 == 0
    inner_rad = lax.axis_index("rad") == 0
    lane = lax.broadcasted_iota(jnp.int32, (radial, LANES), 1)
    parts = count // FIRST_CHUNK

    def part_of(k):
        return fetch((rho_in, vel_in, press_in, nut_in), prim, pl.ds(k * FIRST_CHUNK, FIRST_CHUNK), sems.at[k])

    for k in range(parts):
        for c in part_of(k):
            c.start()
    cols[...] = jnp.zeros(cols.shape, F32)

    def step(a, best):
        speed = 3.0 * sound_speed(prim[0, a], prim[4, a])
        here = lane // 2 == a
        for v in range(6):
            plane = prim[v, a]
            if 1 <= v <= 3:
                speed = speed + jnp.abs(plane)
            high, low = plane[radial - 1 :], plane[:1]
            layer[v, pl.ds(a, 1), :] = jnp.where(inner_rad, high, low)
            far_layer[v, pl.ds(a, 1), :] = jnp.where(inner_rad, low, high)
            first, last = plane[:, :LANES], plane[:, width - LANES :]
            both = pltpu.roll(jnp.where(lane == 0, first, last), 2 * a + 1, 1)
            cols[v] = jnp.where(here, both, cols[v])
        return jnp.maximum(best, speed)

    best = jnp.zeros((radial, width), F32)
    for k in range(parts):
        for c in part_of(k):
            c.wait()
        for j in range(FIRST_CHUNK):
            best = step(k * FIRST_CHUNK + j, best)
    largest = jnp.max(best, axis=0, keepdims=True)
    largest = jnp.max(largest, axis=1, keepdims=True)
    for v in range(6):
        low, high = prim[v, 0], prim[v, count - 1]
        core[v] = jnp.where(even, high, low)
        up_send[v, :, :width] = jnp.where(even, low, high)
        up_send[v, :, width:] = cols[v]
    top[...] = jnp.broadcast_to(largest.reshape(1, 1, 1), top.shape)


def shift_kernel(shift, came, sent, layer, out):
    radial, width = layer.shape[1], layer.shape[2]
    row = lax.axis_index("row")
    amount = shift[0] % width
    amount = jnp.where(row == 1, amount, jnp.where(row == 2, width - amount, 0))
    tiles = amount // LANES
    rest = amount % LANES
    lane = lax.broadcasted_iota(jnp.int32, (radial, LANES), 1)
    for v in range(6):
        parts = [
            pltpu.roll(ref[v, :, h * LANES : (h + 1) * LANES], rest, 1)
            for ref in (came, sent)
            for h in range(2)
        ]
        for t in range(2):
            picks = [
                jnp.where(lane < rest, parts[max(1 + t - q, 0)], parts[2 + t - q]) for q in range(3)
            ]
            out[v, :radial, t * LANES : (t + 1) * LANES] = jnp.where(
                tiles == 0, picks[0], jnp.where(tiles == 1, picks[1], picks[2])
            )
        out[v, radial:, :] = layer[v]


def weight_kernel(fwd, back, own, other, out):
    radial = out.shape[1]
    low = lax.axis_index("rad") == 0
    table = jnp.where(lax.axis_index("row") == 1, fwd[...], back[...])
    for v in range(6):
        mine, theirs = own[v, :radial], other[v, :radial]
        plane = jnp.concatenate([jnp.where(low, mine, theirs), jnp.where(low, theirs, mine)], 0)
        out[v] = jnp.dot(
            table, plane, precision=lax.Precision.HIGHEST, preferred_element_type=F32
        )


def closure(rho, nut, dist, grad2):
    square = jnp.maximum(grad2, GRAD_FLOOR * GRAD_FLOOR)
    inverse = lax.rsqrt(square)
    strain = square * inverse
    eight = (8.0 / (KAPPA * KAPPA)) * (nut + NU_LAM) * inverse / (dist * dist)
    shielding = 1.0 - jnp.tanh(eight * eight * eight)
    length = dist - shielding * jnp.maximum(0.0, dist - C_DES)
    quot = nut / length
    return shielding, rho * (CB1 * strain * nut - CW1 * (quot * quot))


def state_at(prim, der, a):
    return dict(
        rho=prim[0, a],
        u=[prim[1 + i, a] for i in range(3)],
        p=prim[4, a],
        m=[der[i, a] for i in range(3)],
        e=der[3, a],
        n=der[4, a],
        c=der[5, a],
    )


def face_kernel(
    prim, wall_in, core, layer, own_layer, wall_layer, came, col_next,
    col_own, top, flow_out, shield_out, edge_out, tail_out,
    der, wall, flow, shield,
    low_face, lay_hi, lay_lo, lay_u, azi_hi, azi_lo, azi_u, sems, out_sems,
):
    _, count, radial, width = prim.shape
    row, rad = lax.axis_index("row"), lax.axis_index("rad")
    even = row % 2 == 0
    at_low = rad == 0
    parts = count // CHUNK

    def part_of(k):
        rows = pl.ds(k * CHUNK, CHUNK)
        return [pltpu.make_async_copy(wall_in.at[rows], wall.at[rows], sems.at[k])]

    def results_of(k):
        rows = pl.ds(k * CHUNK, CHUNK)
        return [
            pltpu.make_async_copy(flow.at[:, rows], flow_out.at[:, rows], out_sems.at[k, 0]),
            pltpu.make_async_copy(shield.at[rows], shield_out.at[rows], out_sems.at[k, 1]),
        ]

    for k in range(parts):
        for c in part_of(k):
            c.start()
    step_size = CFL / jnp.max(top[...])
    half = 0.5 * step_size
    sub = lax.broadcasted_iota(jnp.int32, (8, width), 0)
    lane = lax.broadcasted_iota(jnp.int32, (radial, LANES), 1)

    def derive(a):
        q = [prim[v, a] for v in range(6)]
        s = state_of(q)
        for i in range(3):
            der[i, a] = s["m"][i]
        der[3, a] = s["e"]
        der[4, a] = s["n"]
        der[5, a] = s["c"]

    def up_r(v, halo):
        lo, hi = pltpu.roll(v[:8], 7, 0), pltpu.roll(v[8:], 7, 0)
        edge = sub == 7
        return jnp.concatenate([jnp.where(edge, hi, lo), jnp.where(edge, halo, hi)], 0)

    def down_r(v, halo):
        lo, hi = pltpu.roll(v[:8], 1, 0), pltpu.roll(v[8:], 1, 0)
        edge = sub == 0
        return jnp.concatenate([jnp.where(edge, halo, lo), jnp.where(edge, lo, hi)], 0)

    def up_t(v, halo):
        lo, hi = pltpu.roll(v[:, :LANES], LANES - 1, 1), pltpu.roll(v[:, LANES:], LANES - 1, 1)
        edge = lane == LANES - 1
        return jnp.concatenate([jnp.where(edge, hi, lo), jnp.where(edge, halo, hi)], 1)

    def down_t(v, halo):
        lo, hi = pltpu.roll(v[:, :LANES], 1, 1), pltpu.roll(v[:, LANES:], 1, 1)
        edge = lane == 0
        return jnp.concatenate([jnp.where(edge, halo, lo), jnp.where(edge, lo, hi)], 1)

    def mirrored(q):
        return [q[0], q[1], -q[2], q[3], q[4], q[5]]

    got = [layer[v, radial:] for v in range(6)]
    bottom = [jnp.where(at_low, wall_layer[v], own_layer[v]) for v in range(6)]
    ceiling = [jnp.where(at_low, own_layer[v], wall_layer[v]) for v in range(6)]
    high = [jnp.where(at_low, g, w) for g, w in zip(got, mirrored(ceiling))]
    low = [jnp.where(at_low, w, g) for g, w in zip(got, mirrored(bottom))]
    high_state = pack_state(state_of(high))
    for i, name in enumerate(PASSED):
        lay_hi[i] = high_state[name]
    for i, f in enumerate(face_of(state_of(low), state_of(bottom), 1)):
        lay_lo[i] = f
    for i in range(3):
        lay_u[i] = low[1 + i]

    def column(ref, v):
        q = ref[v, :, ref.shape[2] - LANES :]
        return jnp.where(lane < 2 * count, q, 1.0)

    nxt_state = pack_state(state_of([column(col_next, v) for v in range(6)]))
    for i, name in enumerate(PASSED):
        azi_hi[i] = nxt_state[name]
    prev = [column(came, v) for v in range(6)]
    for i, f in enumerate(face_of(state_of(prev), state_of([pltpu.roll(column(col_own, v), LANES - 1, 1) for v in range(6)]), 2)):
        azi_lo[i] = f
    for i in range(3):
        azi_u[i] = prev[1 + i]

    end = [core[v] for v in range(6)]
    end_state = state_of(end)
    no_low = jnp.where(even, 0.0, 1.0)
    no_high = jnp.where(even, 1.0, 0.0)
    for c in part_of(0):
        c.wait()
    derive(0)
    for i, f in enumerate(face_of(end_state, state_at(prim, der, 0), 0)):
        low_face[i] = f * no_low

    def step(a, _):
        here = state_at(prim, der, a)
        last = a == count - 1
        first = a == 0
        later = jnp.minimum(a + 1, count - 1)
        earlier = jnp.maximum(a - 1, 0)
        total = [None] * 6
        derive(later)
        above = state_at(prim, der, later)
        right = dict(
            (k, [jnp.where(last, g, h) for g, h in zip(end_state[k], above[k])])
            if isinstance(above[k], list)
            else (k, jnp.where(last, end_state[k], above[k]))
            for k in above
        )
        keep = jnp.where(last, no_high, 1.0)
        for i, f in enumerate(face_of(here, right, 0)):
            f = f * keep
            total[i] = f - low_face[i]
            low_face[i] = f
        grad2 = None
        for i in range(3):
            down = jnp.where(first, end[1 + i], prim[1 + i, earlier])
            d = right["u"][i] - down
            grad2 = d * d if grad2 is None else grad2 + d * d
        outermost = jnp.where(even, first, last)
        grad2 = grad2 * jnp.where(outermost, 0.0, 1.0)
        packed = pack_state(here)
        row_of = pl.ds(a, 1)
        shifted = {n: up_r(packed[n], lay_hi[i, row_of, :]) for i, n in enumerate(PASSED)}
        face = face_of(here, unpack_state(shifted), 1)
        for i, f in enumerate(face):
            total[i] = total[i] + (f - down_r(f, lay_lo[i, row_of, :]))
        for i in range(3):
            d = shifted["u%d" % i] - down_r(here["u"][i], lay_u[i, row_of, :])
            grad2 = grad2 + d * d
        to_end = (LANES - 2) - 2 * a
        to_start = (LANES - 2 * a) % LANES
        shifted = {n: up_t(packed[n], pltpu.roll(azi_hi[i], to_end, 1)) for i, n in enumerate(PASSED)}
        face = face_of(here, unpack_state(shifted), 2)
        for i, f in enumerate(face):
            total[i] = total[i] + (f - down_t(f, pltpu.roll(azi_lo[i], to_start, 1)))
        for i in range(3):
            d = shifted["u%d" % i] - down_t(here["u"][i], pltpu.roll(azi_u[i], to_start, 1))
            grad2 = grad2 + d * d
        shielding, source = closure(here["rho"], prim[5, a], wall[a], 0.25 * grad2)
        cons = cons_of(here)
        for i in range(5):
            flow[i, a] = cons[i] - half * total[i]
        flow[5, a] = cons[5] - half * total[5] + step_size * source
        shield[a] = shielding

        @pl.when(outermost)
        def _():
            for i in range(6):
                edge_out[i] = cons[i] - half * total[i]
            edge_out[6] = grad2
            edge_out[7] = wall[a]
            inside = jnp.where(even, 1, count - 2)
            for i in range(3):
                edge_out[8 + i] = prim[1 + i, inside]
            edge_out[11] = jnp.zeros((radial, width), F32) + step_size

        return 0

    def part_step(k, _):
        @pl.when(k + 1 < parts)
        def _():
            for c in part_of(k + 1):
                c.wait()

        lax.fori_loop(k * CHUNK, (k + 1) * CHUNK, step, 0)
        @pl.when(k + 1 < parts)
        def _():
            for c in results_of(k):
                c.start()

        return 0

    lax.fori_loop(0, parts, part_step, 0)
    for j in range(CHUNK):
        for i in range(6):
            tail_out[i, j] = flow[i, count - CHUNK + j]
        tail_out[6, j] = shield[count - CHUNK + j]
    for k in range(parts - 1):
        for c in results_of(k):
            c.wait()


def edge_kernel(
    flow_in, shield_in, edge, tail, sent, ghost, flow_out, shield_out,
    edge_flow, edge_shield, last_flow, last_shield, sems,
):
    del flow_in, shield_in
    _, radial, width = ghost.shape
    count = shield_out.shape[0]
    row = lax.axis_index("row")
    even = row % 2 == 0
    coupled = (row == 1) | (row == 2)
    step_size = edge[11]
    rows = pl.ds(count - CHUNK, CHUNK - 1)
    copies = [
        pltpu.make_async_copy(
            tail.at[pl.ds(0, 6), pl.ds(0, CHUNK - 1)], flow_out.at[:, rows], sems.at[0]
        ),
        pltpu.make_async_copy(tail.at[6, pl.ds(0, CHUNK - 1)], shield_out.at[rows], sems.at[1]),
    ]
    for c in copies:
        c.start()
    mine = [sent[v, :, :width] for v in range(6)]
    beyond = [jnp.where(coupled, ghost[v], mine[v]) for v in range(6)]
    here, out_state = state_of(mine), ghost_state_of(beyond)
    grad2 = 0.25 * edge[6]
    for i in range(3):
        d = 0.5 * (edge[8 + i] - beyond[1 + i])
        grad2 = grad2 + d * d

    def pick(p, q):
        return dict(
            (k, [jnp.where(even, x, y) for x, y in zip(p[k], q[k])])
            if isinstance(p[k], list)
            else (k, jnp.where(even, p[k], q[k]))
            for k in p
        )

    shielding, source = closure(here["rho"], mine[5], edge[7], grad2)
    edge_shield[...] = shielding
    last_shield[...] = jnp.where(even, tail[6, CHUNK - 1], shielding)
    sign = jnp.where(even, -1.0, 1.0)
    for i, f in enumerate(ghost_face_of(pick(out_state, here), pick(here, out_state), 0)):
        value = edge[i] - step_size * (sign * f)
        if i == 5:
            value = value + step_size * source
        edge_flow[i] = value
        last_flow[i] = jnp.where(even, tail[i, CHUNK - 1], value)
    copies += [
        pltpu.make_async_copy(last_flow, flow_out.at[:, count - 1], sems.at[2]),
        pltpu.make_async_copy(last_shield, shield_out.at[count - 1], sems.at[3]),
    ]
    firsts = [
        pltpu.make_async_copy(edge_flow, flow_out.at[:, 0], sems.at[4]),
        pltpu.make_async_copy(edge_shield, shield_out.at[0], sems.at[5]),
    ]
    for c in copies[2:]:
        c.start()

    @pl.when(even)
    def _():
        for c in firsts:
            c.start()
        for c in firsts:
            c.wait()

    for c in copies:
        c.wait()


def derive_call(fields, devices):
    count, radial, width = fields[0].shape
    plane, layer = shaped(6, radial, width), shaped(6, count, width)
    return pl.pallas_call(
        derive_kernel,
        out_shape=(
            plane, shaped(6, radial, width + LANES), layer, layer, shaped(6, radial, LANES),
            shaped(devices, 1, LANES), pltpu.VMEM((6, count, radial, width), F32),
        ),
        in_specs=[HBM] * 4,
        out_specs=(VMEM,) * 7,
        scratch_shapes=[pltpu.SemaphoreType.DMA((count // FIRST_CHUNK, 4))],
        compiler_params=params(),
        name="derive",
    )(*fields)


def faces_call(*arrays):
    whole = arrays[0].shape
    _, count, radial, width = whole
    parts = count // CHUNK
    return pl.pallas_call(
        face_kernel,
        out_shape=(
            apart(*whole), apart(count, radial, width), shaped(12, radial, width),
            shaped(7, CHUNK, radial, width),
        ),
        in_specs=[VMEM, HBM] + [VMEM] * 8,
        out_specs=(HBM, HBM, VMEM, VMEM),
        scratch_shapes=[
            pltpu.VMEM(whole, F32),
            pltpu.VMEM((count, radial, width), F32),
            pltpu.VMEM(whole, F32),
            pltpu.VMEM((count, radial, width), F32),
            pltpu.VMEM((6, radial, width), F32),
            pltpu.VMEM((8, count, width), F32),
            pltpu.VMEM((6, count, width), F32),
            pltpu.VMEM((3, count, width), F32),
            pltpu.VMEM((8, radial, LANES), F32),
            pltpu.VMEM((6, radial, LANES), F32),
            pltpu.VMEM((3, radial, LANES), F32),
            pltpu.SemaphoreType.DMA((parts,)),
            pltpu.SemaphoreType.DMA((parts, 2)),
        ],
        compiler_params=params(),
        cost_estimate=pl.CostEstimate(
            flops=25_000_000, bytes_accessed=6_000_000, transcendentals=300_000
        ),
        name="faces",
    )(*arrays)


def edge_call(flow, shield, edge, tail, sent, ghost):
    _, radial, width = ghost.shape
    return pl.pallas_call(
        edge_kernel,
        out_shape=(shaped(*flow.shape), shaped(*shield.shape)),
        in_specs=[HBM] * 2 + [VMEM] * 4,
        out_specs=(HBM, HBM),
        input_output_aliases={0: 0, 1: 1},
        scratch_shapes=[
            pltpu.VMEM((6, radial, width), F32),
            pltpu.VMEM((radial, width), F32),
            pltpu.VMEM((6, radial, width), F32),
            pltpu.VMEM((radial, width), F32),
            pltpu.SemaphoreType.DMA((6,)),
        ],
        compiler_params=params(),
        name="edge",
    )(flow, shield, edge, tail, sent, ghost)


def body(density, velocity, pressure, nu_tilde, wall_distance, interp_fwd, interp_back, offset):
    rows, rads, cycle = (lax.axis_size(n) for n in AXES)
    count, radial, width = density.shape

    def device(row, rad, azi):
        return (row * rads + rad) * cycle + azi % cycle

    def everyone(target):
        return [
            (device(r, d, a), target(r, d, a))
            for r in range(rows)
            for d in range(rads)
            for a in range(cycle)
        ]

    plane = shaped(6, radial, width)
    devices = rows * rads * cycle
    fields = [far_away(x) for x in (density, velocity, pressure, nu_tilde)]
    core, up_send, layer, far_layer, cols, top, prim = derive_call(fields, devices)

    up = everyone(lambda r, d, a: device(r, d, a + 1))
    down = everyone(lambda r, d, a: device(r, d, a - 1))
    pair = everyone(lambda r, d, a: device(r ^ 1, d, a))
    across = everyone(lambda r, d, a: device(r, rads - 1 - d, a))
    tops = lax.all_to_all(top, AXES, 0, 0)
    came = lax.ppermute(up_send, AXES, up)
    col_next = lax.ppermute(cols, AXES, down)
    core_got = lax.ppermute(core, AXES, pair)

    moved = pl.pallas_call(
        shift_kernel,
        out_shape=shaped(6, radial + count, width),
        in_specs=[SMEM, VMEM, VMEM, VMEM],
        out_specs=VMEM,
        compiler_params=params(),
        name="shift",
    )(offset, came, up_send, layer)
    swapped = lax.ppermute(moved, AXES, across)
    weighted = pl.pallas_call(
        weight_kernel,
        out_shape=plane,
        in_specs=[VMEM] * 4,
        out_specs=VMEM,
        compiler_params=params(),
        name="weigh",
    )(interp_fwd, interp_back, moved, swapped)

    def far(blocks):
        route = []
        for d in range(rads):
            for a in range(cycle):
                route.append((device(1, d, a), device(2, d, a + blocks)))
                route.append((device(2, d, a), device(1, d, a + cycle - 1 - blocks)))

        def branch(block, sent, near, dist, *rest):
            near = pltpu.with_memory_space_constraint(near, pltpu.VMEM)
            ghost = lax.ppermute(block, AXES, route)
            flow, shield, edge, tail = faces_call(near, far_away(dist), *rest)
            return edge_call(far_away(flow), far_away(shield), edge, tail, sent, ghost)

        return branch

    return lax.switch(
        lax.div(offset[0], width),
        [far(b) for b in range(cycle)],
        weighted, up_send, prim, wall_distance,
        core_got, swapped, layer, far_layer, came, col_next, cols, tops,
    )


def solution(mesh):
    placed = (
        P("row", "rad", "azi"),
        P(None, "row", "rad", "azi"),
        P("row", "rad", "azi"),
        P("row", "rad", "azi"),
        P("row", "rad", "azi"),
        P("rad", None),
        P("rad", None),
        P(),
    )
    return jax.shard_map(
        body,
        mesh=mesh,
        in_specs=placed,
        out_specs=(P(None, "row", "rad", "azi"), P("row", "rad", "azi")),
        check_vma=False,
    )
```
